512 devices in a mesh: inner: 16 (over x, y_hi), outer: 8 (over z), head: 4 (over y_lo, core).
Axes of the slice: x: 4, y: 8 (y_hi: 4, y_lo: 2; y = y_hi * 2 + y_lo), z: 8, core: 2. Of those that a mesh axis runs over, the one named last changes fastest.
Arguments:
- queries: bfloat16 [16384, 24, 128], P(('outer', 'inner'), 'head'), may hold values from -6 to 6
- key_rows: bfloat16 [16384, 4, 128], P(('outer', 'inner'), 'head'), may hold values from -6 to 6
- value_rows: bfloat16 [16384, 4, 128], P(('outer', 'inner'), 'head'), may hold values from -6 to 6
- attn_out: bfloat16 [16384, 24, 128], P(('outer', 'inner'), 'head'), may hold values from -3 to 3
- grad_out: bfloat16 [16384, 24, 128], P(('outer', 'inner'), 'head'), may hold values from -96 to 96
- log_norms: float32 [24, 16384], P('head', ('outer', 'inner'))
- pair_order: int32 [16], replicated, may hold values from 0 to 15, each once
Outputs:
- grad_queries: bfloat16 [16384, 24, 128], P(('outer', 'inner'), 'head')
- grad_keys: bfloat16 [16384, 4, 128], P(('outer', 'inner'), 'head')
- grad_values: bfloat16 [16384, 4, 128], P(('outer', 'inner'), 'head')
The draws below stay inside these ranges and needn't reach their ends.
Inputs may be any that keep to these rules, and one draw needn't show every extreme that they name: Index i of inner holds, in every segment, span pair_order[i] in its first 64 rows and span 32 - 1 - pair_order[i] in its last 64 rows.
All inputs are finite; a program needn't handle non-finite values.
Results may differ from the reference program's by a relative error of at most 0.0053.
Values may be sent and summed in bfloat16 or wider, within the bound.
A program may use at most 64 MiB of HBM per device.

```python
import math
import jax
import jax.numpy as jnp
from jax import lax

SPAN = 64
HEAD_DIM = 128
KV_HEADS = 4
GROUP = 6
Q_HEADS = 24
SEG = 2048
SEQ = 16384
N_INNER = 16
N_OUTER = 8


def draw_log_norms(key, part):
    key = jax.random.fold_in(key, 11)
    base_level = jnp.log(jnp.float32(SEG))
    offset = 1.25 + 0.4 * jax.random.truncated_normal(key, -3.0, 3.0, (Q_HEADS, SEQ), jnp.float32)
    return (base_level + offset).astype(jnp.float32)


def levels(key, shape, cuts, least, high):
    def one(axis_at, shards_of):
        steps = jax.random.uniform(jax.random.fold_in(jax.random.fold_in(key, 6), axis_at), (shards_of,), jnp.float32, least / len(cuts), high / len(cuts))
        return jnp.repeat(jnp.exp(steps), shape[axis_at] // shards_of).reshape((-1,) + (1,) * (len(shape) - axis_at - 1))

    factor_of = one(*cuts[0])
    for cut in cuts[1:]:
        factor_of = factor_of * one(*cut)
    return factor_of


def scatter_about(rng, dims, scale, reach, cuts=(), kind=jnp.bfloat16):
    values = jax.random.normal(rng, dims, jnp.float32) * scale
    if len(cuts) > 0:
        values = levels(rng, dims, cuts, -0.22, 0.18) * values
    return jnp.clip(values, min=-reach, max=reach).astype(kind)


def setup_inputs(seed: int = 0) -> dict:
    seeds = jax.random.split(jax.random.key(seed), 8)
    return {
        "queries": scatter_about(seeds[0], (SEQ, Q_HEADS, HEAD_DIM), 1.0, 6.0, ((0, 128), (1, 4))),
        "key_rows": scatter_about(seeds[1], (SEQ, KV_HEADS, HEAD_DIM), 1.0, 6.0, ((0, 128), (1, 4))),
        "value_rows": scatter_about(seeds[2], (SEQ, KV_HEADS, HEAD_DIM), 1.0, 6.0, ((0, 128), (1, 4))),
        "attn_out": scatter_about(seeds[3], (SEQ, Q_HEADS, HEAD_DIM), 0.5, 3.0, ((0, 128), (1, 4))),
        "grad_out": scatter_about(seeds[4], (SEQ, Q_HEADS, HEAD_DIM), 16.0, 96.0, ((0, 128), (1, 4))),
        "log_norms": draw_log_norms(jax.random.fold_in(seeds[7], 71), 0),
        "pair_order": jax.random.permutation(seeds[6], N_INNER).astype(jnp.int32),
    }


def segment_positions(pair_order, within, span_rows):
    slot_index = within // (2 * span_rows)
    local_rows = within % (2 * span_rows)
    rank_value = jnp.take(pair_order, slot_index)
    span_count = 2 * pair_order.shape[0]
    first_half = rank_value * span_rows + local_rows
    second_half = (span_count - 1 - rank_value) * span_rows + local_rows - span_rows
    return jnp.where(local_rows < span_rows, first_half, second_half).astype(jnp.int32)

def block_grads(queries_five, grad_five, norms_four, dots_four, key_blocks, value_blocks, visible, inv_root):
    queries_wide = queries_five.astype(jnp.float32)
    grad_wide = grad_five.astype(jnp.float32)
    scores = jnp.einsum('arhgd,bkhd->ahgrbk', queries_wide, key_blocks.astype(jnp.float32)) * inv_root
    attn_weights = jnp.where(visible[:, None, None], jnp.exp(scores - norms_four[..., None, None]), 0.0)
    weights_half = attn_weights.astype(jnp.bfloat16)
    grad_weights = jnp.einsum('arhgd,bkhd->ahgrbk', grad_wide, value_blocks.astype(jnp.float32))
    grad_scores = (attn_weights * (grad_weights - dots_four[..., None, None])).astype(jnp.bfloat16)
    score_wide = grad_scores.astype(jnp.float32)
    value_grad = jnp.einsum('ahgrbk,arhgd->bkhd', weights_half.astype(jnp.float32), grad_wide)
    key_grad = jnp.einsum('ahgrbk,arhgd->bkhd', score_wide, queries_wide) * inv_root
    query_grad = jnp.einsum('ahgrbk,bkhd->arhgd', score_wide, key_blocks.astype(jnp.float32)) * inv_root
    return (query_grad, key_grad, value_grad)

def reference(queries, key_rows, value_rows, attn_out, grad_out, log_norms, pair_order):
    inv_root = 1.0 / math.sqrt(HEAD_DIM)
    row_dot = lax.optimization_barrier(jnp.sum(grad_out.astype(jnp.float32) * attn_out.astype(jnp.float32), axis=-1))
    within = jnp.arange(SEG, dtype=jnp.int32)
    positions = segment_positions(pair_order, within, SPAN)
    causal = positions[None, :] <= positions[:, None]
    query_heads = jnp.moveaxis(queries.reshape(SEQ, KV_HEADS, GROUP, HEAD_DIM), 1, 0)
    grad_heads = jnp.moveaxis(grad_out.reshape(SEQ, KV_HEADS, GROUP, HEAD_DIM), 1, 0)
    key_heads = jnp.moveaxis(key_rows, 1, 0)
    value_heads = jnp.moveaxis(value_rows, 1, 0)
    norm_heads = log_norms.reshape(KV_HEADS, GROUP, SEQ)
    dot_heads = row_dot.T.reshape(KV_HEADS, GROUP, SEQ)

    def one_head(operands):
        head_queries, head_grads, head_keys, head_values, head_norms, head_dots = operands
        query_parts = []
        key_parts = [jnp.zeros((SEG, HEAD_DIM), jnp.float32) for segment in range(N_OUTER)]
        value_parts = [jnp.zeros((SEG, HEAD_DIM), jnp.float32) for segment in range(N_OUTER)]
        for segment in range(N_OUTER):
            start_row = segment * SEG
            stop_row = start_row + SEG
            own_keys = head_keys[start_row:stop_row]
            own_values = head_values[start_row:stop_row]
            if segment > 0:
                prev_keys = head_keys[start_row - SEG:start_row]
                prev_values = head_values[start_row - SEG:start_row]
            else:
                prev_keys = jnp.zeros_like(own_keys)
                prev_values = jnp.zeros_like(own_values)
            key_blocks = jnp.stack([prev_keys, own_keys])[:, :, None, :]
            value_blocks = jnp.stack([prev_values, own_values])[:, :, None, :]
            visible = jnp.stack([jnp.full((SEG, SEG), segment > 0), causal], axis=1)[None]
            query_grad, key_grad, value_grad = block_grads(head_queries[start_row:stop_row][None, :, None], head_grads[start_row:stop_row][None, :, None], head_norms[:, start_row:stop_row][None, None], head_dots[:, start_row:stop_row][None, None], key_blocks, value_blocks, visible, inv_root)
            query_parts.append(query_grad[0, :, 0])
            key_parts[segment] = key_parts[segment] + key_grad[1, :, 0]
            value_parts[segment] = value_parts[segment] + value_grad[1, :, 0]
            if segment > 0:
                key_parts[segment - 1] = key_parts[segment - 1] + key_grad[0, :, 0]
                value_parts[segment - 1] = value_parts[segment - 1] + value_grad[0, :, 0]
        return (jnp.concatenate(query_parts), jnp.concatenate(key_parts), jnp.concatenate(value_parts))
    query_grad, key_grad, value_grad = lax.map(one_head, (query_heads, grad_heads, key_heads, value_heads, norm_heads, dot_heads))
    grad_queries = jnp.moveaxis(query_grad, 0, 1).reshape(SEQ, Q_HEADS, HEAD_DIM).astype(jnp.bfloat16)
    grad_keys = jnp.moveaxis(key_grad, 0, 1).astype(jnp.bfloat16)
    grad_values = jnp.moveaxis(value_grad, 0, 1).astype(jnp.bfloat16)
    return (grad_queries, grad_keys, grad_values)
```

```python
import functools
import math

import jax
import jax.numpy as jnp
from jax import lax
from jax.experimental import pallas as pl
from jax.experimental.pallas import tpu as pltpu
from jax.sharding import PartitionSpec as P

MESH = pl.DeviceIdType.MESH
LOG2E = math.log2(math.e)
X_DEVICES = 4
Y_DEVICES = 4
ROWS = 128
HEADS = 6
DIM = 128
SPAN = 64
GROUP_KEYS = Y_DEVICES * ROWS
PAIRS = HEADS // 2
OUTER = 8

NT = (((1,), (1,)), ((), ()))
TN = (((0,), (0,)), ((), ()))
NN = (((1,), (0,)), ((), ()))


def dot(a, b, dims):
    return lax.dot_general(a, b, dims, preferred_element_type=jnp.float32)


def kernel(
    order_ref, q_ref, k_ref, v_ref, o_ref, g_ref, lse_ref,
    dq_ref, dk_ref, dv_ref,
    kv, qs, gs, stat, kpos, weights, scores, dq_acc, acc,
    sx, rx, sy, ry, sq, rq,
    local_sem, z_send, z_recv, ag_send_y, ag_send_x, ag_recv,
    rs_send_x, rs_recv_x, rs_send_y, rs_recv_y, dq_send, dq_recv,
):
    inner = lax.axis_index("inner")
    outer = lax.axis_index("outer")
    head = lax.axis_index("head")
    x = inner // Y_DEVICES
    y = lax.rem(inner, Y_DEVICES)
    inv_root = 1.0 / math.sqrt(DIM)

    def at_x(distance):
        return (lax.rem(x + distance, X_DEVICES) * Y_DEVICES + y, outer, head)

    def at_y(distance):
        return (x * Y_DEVICES + lax.rem(y + distance, Y_DEVICES), outer, head)

    def at_z(distance):
        return (inner, outer + distance, head)

    def block(xi, yi):
        return kv.at[xi, :, pl.ds(pl.multiple_of(yi * ROWS, ROWS), ROWS), :]

    mine = pl.ds(pl.multiple_of(y * ROWS, ROWS), ROWS)
    loads = [
        pltpu.make_async_copy(k_ref, kv.at[x, 0, mine, :], local_sem.at[0]),
        pltpu.make_async_copy(v_ref, kv.at[x, 1, mine, :], local_sem.at[1]),
        pltpu.make_async_copy(q_ref, qs.at[0], local_sem.at[2]),
        pltpu.make_async_copy(g_ref, gs.at[0], local_sem.at[3]),
    ]
    for load in loads:
        load.start()

    barrier = pltpu.get_barrier_semaphore()
    for distance in (1, 2, 3):
        pl.semaphore_signal(barrier, inc=1, device_id=at_x(distance), device_id_type=MESH)
        pl.semaphore_signal(barrier, inc=1, device_id=at_y(distance), device_id_type=MESH)

    @pl.when(outer > 0)
    def _():
        pl.semaphore_signal(barrier, inc=1, device_id=at_z(-1), device_id_type=MESH)

    @pl.when(outer < OUTER - 1)
    def _():
        pl.semaphore_signal(barrier, inc=1, device_id=at_z(1), device_id_type=MESH)

    for load in loads:
        load.wait()

    stat[0, 0, 0:HEADS, :] = lse_ref[...] * LOG2E
    ones = jnp.ones((8, DIM), jnp.bfloat16)
    for h in range(HEADS):
        product = gs[0, h].astype(jnp.float32) * o_ref[h].astype(jnp.float32)
        high = product.astype(jnp.bfloat16)
        low = (product - high.astype(jnp.float32)).astype(jnp.bfloat16)
        sums = dot(ones, high, NT) + dot(ones, low, NT)
        stat[0, 1, h : h + 1, :] = sums[0:1, :]

    peers = 6 + jnp.minimum(outer, 1) + jnp.minimum(OUTER - 1 - outer, 1)
    pl.semaphore_wait(barrier, peers)

    def send_y(distance):
        return pltpu.make_async_remote_copy(
            block(x, y), block(x, y), ag_send_y.at[distance - 1],
            ag_recv.at[x * Y_DEVICES + y], device_id=at_y(distance), device_id_type=MESH,
        )

    def send_x(step, distance):
        yi = lax.rem(y + step, Y_DEVICES)
        return pltpu.make_async_remote_copy(
            block(x, yi), block(x, yi), ag_send_x.at[step, distance - 1],
            ag_recv.at[x * Y_DEVICES + yi], device_id=at_x(distance), device_id_type=MESH,
        )

    def wait_block(xi, yi):
        pltpu.make_async_remote_copy(
            block(xi, yi), block(xi, yi), ag_send_y.at[0],
            ag_recv.at[xi * Y_DEVICES + yi], device_id=at_y(1), device_id_type=MESH,
        ).wait_recv()

    def z_copies():
        return [
            pltpu.make_async_remote_copy(
                ref.at[0], ref.at[1], z_send.at[i], z_recv.at[i],
                device_id=at_z(-1), device_id_type=MESH,
            )
            for i, ref in enumerate((stat, qs, gs))
        ]

    for distance in (1, 3, 2):
        send_y(distance).start()

    @pl.when(outer > 0)
    def _():
        for copy in z_copies():
            copy.start()

    for distance in (1, 3, 2):
        send_x(0, distance).start()

    row = lax.broadcasted_iota(jnp.int32, (SPAN, DIM), 0)
    for device in range(X_DEVICES * Y_DEVICES):
        rank = order_ref[device]
        xi, yi = divmod(device, Y_DEVICES)
        kpos[xi, yi * ROWS : yi * ROWS + SPAN, :] = row + rank * SPAN
        kpos[xi, yi * ROWS + SPAN : (yi + 1) * ROWS, :] = (
            row + (2 * X_DEVICES * Y_DEVICES - 1 - rank) * SPAN
        )
    lane = lax.broadcasted_iota(jnp.int32, (1, ROWS), 1)
    rank = order_ref[inner]
    qpos = jnp.where(
        lane < SPAN,
        rank * SPAN + lane,
        (2 * X_DEVICES * Y_DEVICES - 1 - rank) * SPAN + lane - SPAN,
    )
    qpos = jnp.concatenate([qpos, qpos], axis=1)

    dq_acc[...] = jnp.zeros_like(dq_acc)

    for step in (1, 3, 2):
        wait_block(x, lax.rem(y + step, Y_DEVICES))
        for distance in (1, 3, 2):
            send_x(step, distance).start()

    def tile(xi, half, masked):
        keys = kv[xi, 0]
        values = kv[xi, 1]
        if masked:
            column = kpos[xi]
            column = jnp.concatenate([column, column], axis=1)
        for pair in range(PAIRS):
            two = slice(2 * pair, 2 * pair + 2)
            q_two = qs[half, two].reshape(2 * ROWS, DIM)
            g_two = gs[half, two].reshape(2 * ROWS, DIM)
            norms = jnp.concatenate(
                [stat[half, 0, 2 * pair + i : 2 * pair + i + 1, :] for i in (0, 1)], axis=1
            )
            dots = jnp.concatenate(
                [stat[half, 1, 2 * pair + i : 2 * pair + i + 1, :] for i in (0, 1)], axis=1
            )
            p = jnp.exp2(dot(keys, q_two, NT) * (inv_root * LOG2E) - norms)
            if masked:
                p = jnp.where(column <= qpos, p, 0.0)
            lanes = slice(2 * pair * ROWS, 2 * (pair + 1) * ROWS)
            weights[:, lanes] = p.astype(jnp.bfloat16)
            ds = (p * (dot(values, g_two, NT) - dots)).astype(jnp.bfloat16)
            scores[:, lanes] = ds
            dq_acc[half, lanes, :] += dot(ds, keys, TN)
        grad_k = dot(scores[...], qs[half].reshape(HEADS * ROWS, DIM), NN)
        grad_v = dot(weights[...], gs[half].reshape(HEADS * ROWS, DIM), NN)
        return grad_k, grad_v

    def own_tile(distance):
        xi = lax.rem(x + distance, X_DEVICES)
        grad_k, grad_v = tile(xi, 0, True)
        acc[xi, 0] = grad_k
        acc[xi, 1] = grad_v

    def wait_group(distance):
        xi = lax.rem(x + distance, X_DEVICES)
        for yi in range(Y_DEVICES):
            wait_block(xi, lax.rem(y + yi, Y_DEVICES))

    own_tile(0)
    for distance in (1, 3, 2):
        wait_group(distance)
        own_tile(distance)

    @pl.when(outer < OUTER - 1)
    def _():
        for copy in z_copies():
            copy.wait_recv()

    @pl.when(outer == OUTER - 1)
    def _():
        stat[1] = jnp.zeros_like(stat[1])
        qs[1] = jnp.zeros_like(qs[1])
        gs[1] = jnp.zeros_like(gs[1])

    def next_tile(distance):
        xi = lax.rem(x + distance, X_DEVICES)
        grad_k, grad_v = tile(xi, 1, False)
        return (acc[xi, 0] + grad_k) * inv_root, acc[xi, 1] + grad_v

    def rs_x(distance):
        return pltpu.make_async_remote_copy(
            sx.at[distance - 1], rx.at[distance - 1], rs_send_x.at[distance - 1],
            rs_recv_x.at[distance - 1], device_id=at_x(distance), device_id_type=MESH,
        )

    for distance in (2, 1, 3):
        grad_k, grad_v = next_tile(distance)
        sx[distance - 1, 0] = grad_k.astype(jnp.bfloat16)
        sx[distance - 1, 1] = grad_v.astype(jnp.bfloat16)
        rs_x(distance).start()
    grad_k, grad_v = next_tile(0)
    acc[x, 0] = grad_k
    acc[x, 1] = grad_v

    def dq_copy():
        return pltpu.make_async_remote_copy(
            sq, rq, dq_send, dq_recv, device_id=at_z(1), device_id_type=MESH
        )

    @pl.when(outer < OUTER - 1)
    def _():
        sq[...] = (dq_acc[1] * inv_root).astype(jnp.bfloat16)
        dq_copy().start()

    for distance in (1, 2, 3):
        rs_x(distance).wait_recv()

    def rs_y(distance):
        return pltpu.make_async_remote_copy(
            sy.at[distance - 1], ry.at[distance - 1], rs_send_y.at[distance - 1],
            rs_recv_y.at[distance - 1], device_id=at_y(distance), device_id_type=MESH,
        )

    def over_x(distance):
        yi = lax.rem(y + distance, Y_DEVICES)
        rows = pl.ds(pl.multiple_of(yi * ROWS, ROWS), ROWS)
        total = acc[x, :, rows, :]
        for i in range(X_DEVICES - 1):
            total = total + rx[i, :, rows, :].astype(jnp.float32)
        return total

    for distance in (2, 1, 3):
        sy[distance - 1] = over_x(distance).astype(jnp.bfloat16)
        rs_y(distance).start()
    total = over_x(0)

    @pl.when(outer > 0)
    def _():
        pltpu.make_async_remote_copy(
            sq, rq, dq_send, dq_recv, device_id=at_z(-1), device_id_type=MESH
        ).wait_recv()

    @pl.when(outer == 0)
    def _():
        rq[...] = jnp.zeros_like(rq)

    dq_ref[...] = (
        (dq_acc[0] * inv_root + rq[...].astype(jnp.float32))
        .astype(jnp.bfloat16)
        .reshape(HEADS, ROWS, DIM)
    )

    for distance in (1, 2, 3):
        rs_y(distance).wait_recv()
        total = total + ry[distance - 1].astype(jnp.float32)
    dk_ref[...] = total[0].astype(jnp.bfloat16)
    dv_ref[...] = total[1].astype(jnp.bfloat16)

    for distance in (1, 2, 3):
        send_y(distance).wait_send()
        rs_x(distance).wait_send()
        rs_y(distance).wait_send()
        for step in range(Y_DEVICES):
            send_x(step, distance).wait_send()

    @pl.when(outer > 0)
    def _():
        for copy in z_copies():
            copy.wait_send()

    @pl.when(outer < OUTER - 1)
    def _():
        dq_copy().wait_send()


def on_device(queries, key_rows, value_rows, attn_out, grad_out, log_norms, pair_order):
    def heads_first(rows):
        return jnp.transpose(rows, (1, 0, 2))

    half = jnp.bfloat16
    full = jnp.float32
    dma = pltpu.SemaphoreType.DMA
    vmem = pl.BlockSpec(memory_space=pltpu.VMEM)
    hbm = pl.BlockSpec(memory_space=pl.ANY)
    grad_queries, grad_keys, grad_values = pl.pallas_call(
        kernel,
        out_shape=(
            jax.ShapeDtypeStruct((HEADS, ROWS, DIM), half),
            jax.ShapeDtypeStruct((ROWS, DIM), half),
            jax.ShapeDtypeStruct((ROWS, DIM), half),
        ),
        in_specs=[
            pl.BlockSpec(memory_space=pltpu.SMEM), hbm, hbm, hbm, vmem, hbm, vmem,
        ],
        out_specs=(vmem, vmem, vmem),
        scratch_shapes=[
            pltpu.VMEM((X_DEVICES, 2, GROUP_KEYS, DIM), half),
            pltpu.VMEM((2, HEADS, ROWS, DIM), half),
            pltpu.VMEM((2, HEADS, ROWS, DIM), half),
            pltpu.VMEM((2, 2, 8, ROWS), full),
            pltpu.VMEM((X_DEVICES, GROUP_KEYS, DIM), jnp.int32),
            pltpu.VMEM((GROUP_KEYS, HEADS * ROWS), half),
            pltpu.VMEM((GROUP_KEYS, HEADS * ROWS), half),
            pltpu.VMEM((2, HEADS * ROWS, DIM), full),
            pltpu.VMEM((X_DEVICES, 2, GROUP_KEYS, DIM), full),
            pltpu.VMEM((3, 2, GROUP_KEYS, DIM), half),
            pltpu.VMEM((3, 2, GROUP_KEYS, DIM), half),
            pltpu.VMEM((3, 2, ROWS, DIM), half),
            pltpu.VMEM((3, 2, ROWS, DIM), half),
            pltpu.VMEM((HEADS * ROWS, DIM), half),
            pltpu.VMEM((HEADS * ROWS, DIM), half),
            dma((4,)), dma((3,)), dma((3,)), dma((3,)), dma((4, 3)), dma((16,)),
            dma((3,)), dma((3,)), dma((3,)), dma((3,)), dma, dma,
        ],
        compiler_params=pltpu.CompilerParams(
            collective_id=0, has_side_effects=True, vmem_limit_bytes=60 * 2**20
        ),
        cost_estimate=pl.CostEstimate(
            flops=4 * 10**9, bytes_accessed=10**6, transcendentals=3 * 10**6
        ),
    )(
        pair_order,
        heads_first(queries),
        key_rows.reshape(ROWS, DIM),
        value_rows.reshape(ROWS, DIM),
        heads_first(attn_out),
        heads_first(grad_out),
        log_norms,
    )
    return (
        jnp.transpose(grad_queries, (1, 0, 2)),
        grad_keys.reshape(ROWS, 1, DIM),
        grad_values.reshape(ROWS, 1, DIM),
    )


def solution(mesh):
    rows = P(("outer", "inner"), "head", None)
    return jax.shard_map(
        on_device,
        mesh=mesh,
        in_specs=(rows, rows, rows, rows, rows, P("head", ("outer", "inner")), P()),
        out_specs=(rows, rows, rows),
        check_vma=False,
    )
```

```python
import functools
import math

import jax
import jax.numpy as jnp
from jax import lax
from jax.experimental import pallas as pl
from jax.experimental.pallas import tpu as pltpu
from jax.sharding import PartitionSpec as P

MESH = pl.DeviceIdType.MESH
LOG2E = math.log2(math.e)
X_DEVICES = 4
Y_DEVICES = 4
ROWS = 128
HEADS = 6
DIM = 128
SPAN = 64
GROUP_KEYS = Y_DEVICES * ROWS
PAIRS = HEADS // 2
OUTER = 8

NT = (((1,), (1,)), ((), ()))
TN = (((0,), (0,)), ((), ()))
NN = (((1,), (0,)), ((), ()))


def dot(a, b, dims):
    return lax.dot_general(a, b, dims, preferred_element_type=jnp.float32)


def kernel(
    order_ref, q_ref, k_ref, v_ref, o_ref, g_ref, lse_ref,
    dq_ref, dk_ref, dv_ref,
    kv, qs, gs, attn, lse, stat, kpos, weights, own_scores, next_scores, acc,
    sx, rx, sy, ry, sq, rq,
    local_sem, z_send, z_recv, ag_send_y, ag_send_x, ag_recv,
    rs_send_x, rs_recv_x, rs_send_y, rs_recv_y, dq_send, dq_recv,
):
    inner = lax.axis_index("inner")
    outer = lax.axis_index("outer")
    head = lax.axis_index("head")
    x = inner // Y_DEVICES
    y = lax.rem(inner, Y_DEVICES)
    inv_root = 1.0 / math.sqrt(DIM)

    def at_x(distance):
        return (lax.rem(x + distance, X_DEVICES) * Y_DEVICES + y, outer, head)

    def at_y(distance):
        return (x * Y_DEVICES + lax.rem(y + distance, Y_DEVICES), outer, head)

    def at_z(distance):
        return (inner, outer + distance, head)

    def rows_of(xi):
        return pl.ds(pl.multiple_of(xi * ROWS, ROWS), ROWS)

    def block(xi, yi):
        return kv.at[yi, :, rows_of(xi), :]

    loads = [
        pltpu.make_async_copy(k_ref, kv.at[y, 0, rows_of(x), :], local_sem.at[0]),
        pltpu.make_async_copy(v_ref, kv.at[y, 1, rows_of(x), :], local_sem.at[1]),
        pltpu.make_async_copy(g_ref, gs.at[0], local_sem.at[2]),
        pltpu.make_async_copy(o_ref, attn, local_sem.at[3]),
        pltpu.make_async_copy(lse_ref, lse, local_sem.at[4]),
        pltpu.make_async_copy(q_ref, qs.at[0], local_sem.at[5]),
    ]
    for load in loads:
        load.start()

    barrier = pltpu.get_barrier_semaphore()
    for distance in (1, 2, 3):
        pl.semaphore_signal(barrier, inc=1, device_id=at_x(distance), device_id_type=MESH)
        pl.semaphore_signal(barrier, inc=1, device_id=at_y(distance), device_id_type=MESH)

    @pl.when(outer > 0)
    def _():
        pl.semaphore_signal(barrier, inc=1, device_id=at_z(-1), device_id_type=MESH)

    @pl.when(outer < OUTER - 1)
    def _():
        pl.semaphore_signal(barrier, inc=1, device_id=at_z(1), device_id_type=MESH)

    for load in loads:
        load.wait()

    stat[0, 0, 0:HEADS, :] = lse[...] * LOG2E
    ones = jnp.ones((8, DIM), jnp.bfloat16)
    for h in range(HEADS):
        product = gs[0, h].astype(jnp.float32) * attn[h].astype(jnp.float32)
        high = product.astype(jnp.bfloat16)
        low = (product - high.astype(jnp.float32)).astype(jnp.bfloat16)
        sums = dot(ones, high, NT) + dot(ones, low, NT)
        stat[0, 1, h : h + 1, :] = sums[0:1, :]

    row = lax.broadcasted_iota(jnp.int32, (SPAN, DIM), 0)
    for device in range(X_DEVICES * Y_DEVICES):
        rank = order_ref[device]
        xi, yi = divmod(device, Y_DEVICES)
        kpos[yi, xi * ROWS : xi * ROWS + SPAN, :] = row + rank * SPAN
        kpos[yi, xi * ROWS + SPAN : (xi + 1) * ROWS, :] = (
            row + (2 * X_DEVICES * Y_DEVICES - 1 - rank) * SPAN
        )
    lane = lax.broadcasted_iota(jnp.int32, (1, ROWS), 1)
    rank = order_ref[inner]
    qpos = jnp.where(
        lane < SPAN,
        rank * SPAN + lane,
        (2 * X_DEVICES * Y_DEVICES - 1 - rank) * SPAN + lane - SPAN,
    )
    qpos = jnp.concatenate([qpos, qpos], axis=1)

    peers = 6 + jnp.minimum(outer, 1) + jnp.minimum(OUTER - 1 - outer, 1)
    pl.semaphore_wait(barrier, peers)

    def send_y(distance):
        return pltpu.make_async_remote_copy(
            block(x, y), block(x, y), ag_send_y.at[distance - 1],
            ag_recv.at[x * Y_DEVICES + y], device_id=at_y(distance), device_id_type=MESH,
        )

    def send_x(step, distance):
        yi = lax.rem(y + step, Y_DEVICES)
        return pltpu.make_async_remote_copy(
            block(x, yi), block(x, yi), ag_send_x.at[step, distance - 1],
            ag_recv.at[x * Y_DEVICES + yi], device_id=at_x(distance), device_id_type=MESH,
        )

    def wait_block(xi, yi):
        pltpu.make_async_remote_copy(
            block(xi, yi), block(xi, yi), ag_send_y.at[0],
            ag_recv.at[xi * Y_DEVICES + yi], device_id=at_y(1), device_id_type=MESH,
        ).wait_recv()

    def z_copies():
        return [
            pltpu.make_async_remote_copy(
                ref.at[0], ref.at[1], z_send.at[i], z_recv.at[i],
                device_id=at_z(-1), device_id_type=MESH,
            )
            for i, ref in enumerate((stat, qs, gs))
        ]

    for distance in (1, 3, 2):
        send_y(distance).start()

    for distance in (1, 3, 2):
        send_x(0, distance).start()

    @pl.when(outer > 0)
    def _():
        for copy in z_copies():
            copy.start()

    def tile(step, half, scores):
        yi = lax.rem(y + step, Y_DEVICES)
        keys = kv[yi, 0]
        values = kv[yi, 1]
        if half == 0:
            column = kpos[yi]
            column = jnp.concatenate([column, column], axis=1)
        for pair in range(PAIRS):
            two = slice(2 * pair, 2 * pair + 2)
            q_two = qs[half, two].reshape(2 * ROWS, DIM)
            g_two = gs[half, two].reshape(2 * ROWS, DIM)
            norms = jnp.concatenate(
                [stat[half, 0, 2 * pair + i : 2 * pair + i + 1, :] for i in (0, 1)], axis=1
            )
            dots = jnp.concatenate(
                [stat[half, 1, 2 * pair + i : 2 * pair + i + 1, :] for i in (0, 1)], axis=1
            )
            p = jnp.exp2(dot(keys, q_two, NT) * (inv_root * LOG2E) - norms)
            if half == 0:
                p = jnp.where(column <= qpos, p, 0.0)
            lanes = slice(2 * pair * ROWS, 2 * (pair + 1) * ROWS)
            weights[:, lanes] = p.astype(jnp.bfloat16)
            ds = (p * (dot(values, g_two, NT) - dots)).astype(jnp.bfloat16)
            scores[step, :, lanes] = ds
        grad_k = dot(scores[step], qs[half].reshape(HEADS * ROWS, DIM), NN)
        grad_v = dot(weights[...], gs[half].reshape(HEADS * ROWS, DIM), NN)
        return grad_k, grad_v

    def own_tile(step):
        grad_k, grad_v = tile(step, 0, own_scores)
        acc[step, 0] = grad_k
        acc[step, 1] = grad_v

    def query_grads(scores):
        total = jnp.zeros((HEADS * ROWS, DIM), jnp.float32)
        for step in range(Y_DEVICES):
            total = total + dot(scores[step], kv[lax.rem(y + step, Y_DEVICES), 0], TN)
        return total * inv_root

    def pass_on(step):
        wait_block(x, lax.rem(y + step, Y_DEVICES))
        for distance in (1, 3, 2):
            send_x(step, distance).start()

    def wait_others(step):
        for distance in (1, 3, 2):
            wait_block(lax.rem(x + distance, X_DEVICES), lax.rem(y + step, Y_DEVICES))

    pass_on(1)
    pass_on(3)
    wait_others(0)
    own_tile(0)
    pass_on(2)
    for step in (1, 3, 2):
        wait_others(step)
        own_tile(step)

    @pl.when(outer < OUTER - 1)
    def _():
        for copy in z_copies():
            copy.wait_recv()

    @pl.when(outer == OUTER - 1)
    def _():
        stat[1] = jnp.zeros_like(stat[1])
        qs[1] = jnp.zeros_like(qs[1])
        gs[1] = jnp.zeros_like(gs[1])

    def rs_x(step, distance):
        xi = lax.rem(x + distance, X_DEVICES)
        return pltpu.make_async_remote_copy(
            sx.at[step, :, rows_of(xi), :], rx.at[step, distance - 1],
            rs_send_x.at[step, distance - 1], rs_recv_x.at[step, distance - 1],
            device_id=at_x(distance), device_id_type=MESH,
        )

    def rs_y(step):
        return pltpu.make_async_remote_copy(
            sy.at[step - 1], ry.at[step - 1], rs_send_y.at[step - 1],
            rs_recv_y.at[step - 1], device_id=at_y(step), device_id_type=MESH,
        )

    def next_tile(step):
        grad_k, grad_v = tile(step, 1, next_scores)
        grad_k = (acc[step, 0] + grad_k) * inv_root
        grad_v = acc[step, 1] + grad_v
        acc[step, 0] = grad_k
        acc[step, 1] = grad_v
        sx[step, 0] = grad_k.astype(jnp.bfloat16)
        sx[step, 1] = grad_v.astype(jnp.bfloat16)
        for distance in (2, 1, 3):
            rs_x(step, distance).start()

    def over_x(step):
        total = acc[step, :, rows_of(x), :]
        for distance in (1, 2, 3):
            rs_x(step, distance).wait_recv()
            total = total + rx[step, distance - 1].astype(jnp.float32)
        return total

    def to_y(step):
        sy[step - 1] = over_x(step).astype(jnp.bfloat16)
        rs_y(step).start()

    next_tile(2)
    next_tile(1)
    next_tile(3)
    to_y(2)
    next_tile(0)
    to_y(1)

    def dq_copy(distance):
        return pltpu.make_async_remote_copy(
            sq, rq, dq_send, dq_recv, device_id=at_z(distance), device_id_type=MESH
        )

    sq[...] = query_grads(next_scores).astype(jnp.bfloat16)

    @pl.when(outer < OUTER - 1)
    def _():
        dq_copy(1).start()

    to_y(3)
    total = over_x(0)
    own = query_grads(own_scores)

    @pl.when(outer > 0)
    def _():
        dq_copy(-1).wait_recv()

    @pl.when(outer == 0)
    def _():
        rq[...] = jnp.zeros_like(rq)

    dq_ref[...] = (
        (own + rq[...].astype(jnp.float32)).astype(jnp.bfloat16).reshape(HEADS, ROWS, DIM)
    )

    for step in (1, 2, 3):
        rs_y(step).wait_recv()
        total = total + ry[step - 1].astype(jnp.float32)
    dk_ref[...] = total[0].astype(jnp.bfloat16)
    dv_ref[...] = total[1].astype(jnp.bfloat16)

    for distance in (1, 2, 3):
        send_y(distance).wait_send()
        rs_y(distance).wait_send()
        for step in range(Y_DEVICES):
            send_x(step, distance).wait_send()
            rs_x(step, distance).wait_send()

    @pl.when(outer > 0)
    def _():
        for copy in z_copies():
            copy.wait_send()

    @pl.when(outer < OUTER - 1)
    def _():
        dq_copy(1).wait_send()


def store_kernel(dq_in, dk_in, dv_in, dq_ref, dk_ref, dv_ref, sems):
    copies = [
        pltpu.make_async_copy(dq_in, dq_ref, sems.at[0]),
        pltpu.make_async_copy(dk_in, dk_ref, sems.at[1]),
        pltpu.make_async_copy(dv_in, dv_ref, sems.at[2]),
    ]
    for copy in copies:
        copy.start()
    for copy in copies:
        copy.wait()


def on_device(queries, key_rows, value_rows, attn_out, grad_out, log_norms, pair_order):
    def heads_first(rows):
        return jnp.transpose(rows, (1, 0, 2))

    half = jnp.bfloat16
    full = jnp.float32
    dma = pltpu.SemaphoreType.DMA
    vmem = pl.BlockSpec(memory_space=pltpu.VMEM)
    hbm = pl.BlockSpec(memory_space=pltpu.HBM)
    grads = (
        jax.ShapeDtypeStruct((HEADS, ROWS, DIM), half),
        jax.ShapeDtypeStruct((ROWS, DIM), half),
        jax.ShapeDtypeStruct((ROWS, DIM), half),
    )
    parts = pl.pallas_call(
        kernel,
        out_shape=grads,
        in_specs=[pl.BlockSpec(memory_space=pltpu.SMEM), hbm, hbm, hbm, hbm, hbm, hbm],
        out_specs=(vmem, vmem, vmem),
        scratch_shapes=[
            pltpu.VMEM((Y_DEVICES, 2, GROUP_KEYS, DIM), half),
            pltpu.VMEM((2, HEADS, ROWS, DIM), half),
            pltpu.VMEM((2, HEADS, ROWS, DIM), half),
            pltpu.VMEM((HEADS, ROWS, DIM), half),
            pltpu.VMEM((HEADS, ROWS), full),
            pltpu.VMEM((2, 2, 8, ROWS), full),
            pltpu.VMEM((Y_DEVICES, GROUP_KEYS, DIM), jnp.int32),
            pltpu.VMEM((GROUP_KEYS, HEADS * ROWS), half),
            pltpu.VMEM((Y_DEVICES, GROUP_KEYS, HEADS * ROWS), half),
            pltpu.VMEM((Y_DEVICES, GROUP_KEYS, HEADS * ROWS), half),
            pltpu.VMEM((Y_DEVICES, 2, GROUP_KEYS, DIM), full),
            pltpu.VMEM((Y_DEVICES, 2, GROUP_KEYS, DIM), half),
            pltpu.VMEM((Y_DEVICES, 3, 2, ROWS, DIM), half),
            pltpu.VMEM((3, 2, ROWS, DIM), half),
            pltpu.VMEM((3, 2, ROWS, DIM), half),
            pltpu.VMEM((HEADS * ROWS, DIM), half),
            pltpu.VMEM((HEADS * ROWS, DIM), half),
            dma((6,)), dma((3,)), dma((3,)), dma((3,)), dma((4, 3)), dma((16,)),
            dma((4, 3)), dma((4, 3)), dma((3,)), dma((3,)), dma, dma,
        ],
        compiler_params=pltpu.CompilerParams(
            collective_id=0, has_side_effects=True, vmem_limit_bytes=60 * 2**20
        ),
        cost_estimate=pl.CostEstimate(
            flops=4 * 10**9, bytes_accessed=10**6, transcendentals=3 * 10**6
        ),
    )(
        pair_order,
        heads_first(queries),
        key_rows.reshape(ROWS, DIM),
        value_rows.reshape(ROWS, DIM),
        heads_first(attn_out),
        heads_first(grad_out),
        log_norms,
    )
    grad_queries, grad_keys, grad_values = pl.pallas_call(
        store_kernel,
        out_shape=grads,
        in_specs=[vmem, vmem, vmem],
        out_specs=(hbm, hbm, hbm),
        scratch_shapes=[dma((3,))],
    )(*parts)
    return (
        jnp.transpose(grad_queries, (1, 0, 2)),
        grad_keys.reshape(ROWS, 1, DIM),
        grad_values.reshape(ROWS, 1, DIM),
    )


def solution(mesh):
    rows = P(("outer", "inner"), "head", None)
    return jax.shard_map(
        on_device,
        mesh=mesh,
        in_specs=(rows, rows, rows, rows, rows, P("head", ("outer", "inner")), P()),
        out_specs=(rows, rows, rows),
        check_vma=False,
    )
```

```python
import functools
import math

import jax
import jax.numpy as jnp
from jax import lax
from jax.experimental import pallas as pl
from jax.experimental.pallas import tpu as pltpu
from jax.sharding import PartitionSpec as P

MESH = pl.DeviceIdType.MESH
LOG2E = math.log2(math.e)
X_DEVICES = 4
Y_DEVICES = 4
ROWS = 128
HEADS = 6
DIM = 128
SPAN = 64
GROUP_KEYS = Y_DEVICES * ROWS
PAIRS = HEADS // 2
OUTER = 8

NT = (((1,), (1,)), ((), ()))
TN = (((0,), (0,)), ((), ()))
NN = (((1,), (0,)), ((), ()))


def dot(a, b, dims):
    return lax.dot_general(a, b, dims, preferred_element_type=jnp.float32)


def kernel(
    order_ref, q_ref, k_ref, v_ref, o_ref, g_ref, lse_ref,
    dq_ref, dk_ref, dv_ref,
    kv, qs, gs, attn, lse, stat, kpos, weights, own_scores, next_scores, acc, dq_next,
    sx, rx, sy, ry, sq, rq, dq_out, dkv_out,
    local_sem, z_send, z_recv, ag_send_y, ag_send_own, ag_send_x, ag_recv,
    rs_send_x, rs_recv_x, rs_send_y, rs_recv_y, dq_send, dq_recv,
):
    inner = lax.axis_index("inner")
    outer = lax.axis_index("outer")
    head = lax.axis_index("head")
    x = inner // Y_DEVICES
    y = lax.rem(inner, Y_DEVICES)
    inv_root = 1.0 / math.sqrt(DIM)

    def at_x(distance):
        return (lax.rem(x + distance, X_DEVICES) * Y_DEVICES + y, outer, head)

    def at_y(distance):
        return (x * Y_DEVICES + lax.rem(y + distance, Y_DEVICES), outer, head)

    def at_z(distance):
        return (inner, outer + distance, head)

    def rows_of(xi):
        return pl.ds(pl.multiple_of(xi * ROWS, ROWS), ROWS)

    def block(xi, yi, i):
        return kv.at[yi, i, rows_of(xi), :]

    loads = [
        pltpu.make_async_copy(k_ref, kv.at[y, 0, rows_of(x), :], local_sem.at[0]),
        pltpu.make_async_copy(v_ref, kv.at[y, 1, rows_of(x), :], local_sem.at[1]),
        pltpu.make_async_copy(g_ref, gs.at[0], local_sem.at[2]),
        pltpu.make_async_copy(o_ref, attn, local_sem.at[3]),
        pltpu.make_async_copy(lse_ref, lse, local_sem.at[4]),
        pltpu.make_async_copy(q_ref, qs.at[0], local_sem.at[5]),
    ]
    for load in loads:
        load.start()

    barrier = pltpu.get_barrier_semaphore()
    for distance in (1, 2, 3):
        pl.semaphore_signal(barrier, inc=1, device_id=at_x(distance), device_id_type=MESH)
        pl.semaphore_signal(barrier, inc=1, device_id=at_y(distance), device_id_type=MESH)

    @pl.when(outer > 0)
    def _():
        pl.semaphore_signal(barrier, inc=1, device_id=at_z(-1), device_id_type=MESH)

    @pl.when(outer < OUTER - 1)
    def _():
        pl.semaphore_signal(barrier, inc=1, device_id=at_z(1), device_id_type=MESH)

    peers = 6 + jnp.minimum(outer, 1) + jnp.minimum(OUTER - 1 - outer, 1)
    pl.semaphore_wait(barrier, peers)

    def send_own(i, target, sems, slot):
        return pltpu.make_async_remote_copy(
            (k_ref, v_ref)[i], block(x, y, i), sems.at[slot, i],
            ag_recv.at[x * Y_DEVICES + y, i], device_id=target, device_id_type=MESH,
        )

    def send_y(distance, i):
        return send_own(i, at_y(distance), ag_send_y, distance - 1)

    def send_x(step, distance, i):
        if step == 0:
            return send_own(i, at_x(distance), ag_send_own, distance - 1)
        yi = lax.rem(y + step, Y_DEVICES)
        return pltpu.make_async_remote_copy(
            block(x, yi, i), block(x, yi, i), ag_send_x.at[step - 1, distance - 1, i],
            ag_recv.at[x * Y_DEVICES + yi, i], device_id=at_x(distance), device_id_type=MESH,
        )

    def wait_block(xi, yi, i):
        pltpu.make_async_remote_copy(
            block(xi, yi, i), block(xi, yi, i), ag_send_y.at[0, 0],
            ag_recv.at[xi * Y_DEVICES + yi, i], device_id=at_y(1), device_id_type=MESH,
        ).wait_recv()

    def z_copies():
        return [
            pltpu.make_async_remote_copy(
                source, landing.at[1], z_send.at[i], z_recv.at[i],
                device_id=at_z(-1), device_id_type=MESH,
            )
            for i, (source, landing) in enumerate(((q_ref, qs), (g_ref, gs), (stat.at[0], stat)))
        ]

    @pl.when(outer > 0)
    def _():
        for copy in z_copies()[:2]:
            copy.start()

    for i in (0, 1):
        for distance in (1, 3, 2):
            send_y(distance, i).start()

    for i in (0, 1):
        for distance in (1, 3, 2):
            send_x(0, distance, i).start()

    for load in loads:
        load.wait()

    stat[0, 0, 0:HEADS, :] = lse[...] * LOG2E
    ones = jnp.ones((8, DIM), jnp.bfloat16)
    for h in range(HEADS):
        product = gs[0, h].astype(jnp.float32) * attn[h].astype(jnp.float32)
        high = product.astype(jnp.bfloat16)
        low = (product - high.astype(jnp.float32)).astype(jnp.bfloat16)
        sums = dot(ones, high, NT) + dot(ones, low, NT)
        stat[0, 1, h : h + 1, :] = sums[0:1, :]

    row = lax.broadcasted_iota(jnp.int32, (SPAN, DIM), 0)
    for device in range(X_DEVICES * Y_DEVICES):
        rank = order_ref[device]
        xi, yi = divmod(device, Y_DEVICES)
        kpos[yi, xi * ROWS : xi * ROWS + SPAN, :] = row + rank * SPAN
        kpos[yi, xi * ROWS + SPAN : (xi + 1) * ROWS, :] = (
            row + (2 * X_DEVICES * Y_DEVICES - 1 - rank) * SPAN
        )
    lane = lax.broadcasted_iota(jnp.int32, (1, ROWS), 1)
    rank = order_ref[inner]
    qpos = jnp.where(
        lane < SPAN,
        rank * SPAN + lane,
        (2 * X_DEVICES * Y_DEVICES - 1 - rank) * SPAN + lane - SPAN,
    )
    qpos = jnp.concatenate([qpos, qpos], axis=1)

    @pl.when(outer > 0)
    def _():
        z_copies()[2].start()

    def tile(step, half, scores):
        yi = lax.rem(y + step, Y_DEVICES)
        keys = kv[yi, 0]
        values = kv[yi, 1]
        if half == 0:
            column = kpos[yi]
            column = jnp.concatenate([column, column], axis=1)
        for pair in range(PAIRS):
            two = slice(2 * pair, 2 * pair + 2)
            q_two = qs[half, two].reshape(2 * ROWS, DIM)
            g_two = gs[half, two].reshape(2 * ROWS, DIM)
            norms = jnp.concatenate(
                [stat[half, 0, 2 * pair + i : 2 * pair + i + 1, :] for i in (0, 1)], axis=1
            )
            dots = jnp.concatenate(
                [stat[half, 1, 2 * pair + i : 2 * pair + i + 1, :] for i in (0, 1)], axis=1
            )
            p = jnp.exp2(dot(keys, q_two, NT) * (inv_root * LOG2E) - norms)
            if half == 0:
                p = jnp.where(column <= qpos, p, 0.0)
            lanes = slice(2 * pair * ROWS, 2 * (pair + 1) * ROWS)
            weights[:, lanes] = p.astype(jnp.bfloat16)
            ds = (p * (dot(values, g_two, NT) - dots)).astype(jnp.bfloat16)
            scores[step, :, lanes] = ds

    def key_grad(step, half, i):
        if i == 0:
            scores = (own_scores, next_scores)[half]
            return dot(scores[step], qs[half].reshape(HEADS * ROWS, DIM), NN)
        return dot(weights[...], gs[half].reshape(HEADS * ROWS, DIM), NN)

    def own_tile(step):
        tile(step, 0, own_scores)
        for i in (0, 1):
            acc[step, i] = key_grad(step, 0, i)

    def query_grads(scores, steps):
        total = None
        for step in steps:
            part = dot(scores[step], kv[lax.rem(y + step, Y_DEVICES), 0], TN)
            total = part if total is None else total + part
        return total

    def pass_on(step):
        for i in (0, 1):
            wait_block(x, lax.rem(y + step, Y_DEVICES), i)
            for distance in (1, 3, 2):
                send_x(step, distance, i).start()

    def wait_others(step):
        for i in (0, 1):
            for distance in (1, 3, 2):
                wait_block(lax.rem(x + distance, X_DEVICES), lax.rem(y + step, Y_DEVICES), i)

    def rs_x(step, distance, i):
        xi = lax.rem(x + distance, X_DEVICES)
        return pltpu.make_async_remote_copy(
            sx.at[step, i, rows_of(xi), :], rx.at[step, distance - 1, i],
            rs_send_x.at[step, distance - 1, i], rs_recv_x.at[step, distance - 1, i],
            device_id=at_x(distance), device_id_type=MESH,
        )

    def rs_y(step, i):
        return pltpu.make_async_remote_copy(
            sy.at[step - 1, i], ry.at[step - 1, i], rs_send_y.at[step - 1, i],
            rs_recv_y.at[step - 1, i], device_id=at_y(step), device_id_type=MESH,
        )

    def next_tile(step):
        tile(step, 1, next_scores)
        for i in (0, 1):
            grad = acc[step, i] + key_grad(step, 1, i)
            if i == 0:
                grad = grad * inv_root
            acc[step, i] = grad
            sx[step, i] = grad.astype(jnp.bfloat16)
            for distance in (2, 1, 3):
                rs_x(step, distance, i).start()

    def over_x(step, i):
        total = acc[step, i, rows_of(x), :]
        for distance in (1, 2, 3):
            rs_x(step, distance, i).wait_recv()
            total = total + rx[step, distance - 1, i].astype(jnp.float32)
        return total

    def to_y(step):
        for i in (0, 1):
            sy[step - 1, i] = over_x(step, i).astype(jnp.bfloat16)
            rs_y(step, i).start()

    def dq_copy(distance):
        return pltpu.make_async_remote_copy(
            sq, rq, dq_send, dq_recv, device_id=at_z(distance), device_id_type=MESH
        )

    def store(i):
        return pltpu.make_async_copy(
            (dq_out, dkv_out.at[0], dkv_out.at[1])[i], (dq_ref, dk_ref, dv_ref)[i],
            local_sem.at[i],
        )

    pass_on(1)
    pass_on(3)
    wait_others(0)
    own_tile(0)
    pass_on(2)
    wait_others(1)
    own_tile(1)

    @pl.when(outer < OUTER - 1)
    def _():
        for copy in z_copies():
            copy.wait_recv()

    @pl.when(outer == OUTER - 1)
    def _():
        stat[1] = jnp.zeros_like(stat[1])
        qs[1] = jnp.zeros_like(qs[1])
        gs[1] = jnp.zeros_like(gs[1])

    next_tile(1)
    wait_others(3)
    own_tile(3)
    wait_others(2)
    own_tile(2)
    next_tile(2)
    next_tile(3)
    to_y(1)
    dq_next[...] = query_grads(next_scores, (2, 1, 3))
    next_tile(0)
    sq[...] = (
        (dq_next[...] + query_grads(next_scores, (0,))) * inv_root
    ).astype(jnp.bfloat16)

    @pl.when(outer < OUTER - 1)
    def _():
        dq_copy(1).start()

    to_y(2)
    to_y(3)
    totals = [over_x(0, 0), over_x(0, 1)]
    own = query_grads(own_scores, range(Y_DEVICES)) * inv_root

    @pl.when(outer > 0)
    def _():
        dq_copy(-1).wait_recv()

    @pl.when(outer == 0)
    def _():
        rq[...] = jnp.zeros_like(rq)

    dq_out[...] = (
        (own + rq[...].astype(jnp.float32)).astype(jnp.bfloat16).reshape(HEADS, ROWS, DIM)
    )
    store(0).start()

    for i in (0, 1):
        total = totals[i]
        for step in (1, 3, 2):
            rs_y(step, i).wait_recv()
            total = total + ry[step - 1, i].astype(jnp.float32)
        dkv_out[i] = total.astype(jnp.bfloat16)
        store(1 + i).start()

    for i in (0, 1):
        for distance in (1, 2, 3):
            send_y(distance, i).wait_send()
            rs_y(distance, i).wait_send()
            for step in range(Y_DEVICES):
                send_x(step, distance, i).wait_send()
                rs_x(step, distance, i).wait_send()

    @pl.when(outer > 0)
    def _():
        for copy in z_copies():
            copy.wait_send()

    @pl.when(outer < OUTER - 1)
    def _():
        dq_copy(1).wait_send()

    for i in range(3):
        store(i).wait()


def store_kernel(dq_in, dk_in, dv_in, dq_ref, dk_ref, dv_ref, sems):
    copies = [
        pltpu.make_async_copy(dq_in, dq_ref, sems.at[0]),
        pltpu.make_async_copy(dk_in, dk_ref, sems.at[1]),
        pltpu.make_async_copy(dv_in, dv_ref, sems.at[2]),
    ]
    for copy in copies:
        copy.start()
    for copy in copies:
        copy.wait()


def on_device(queries, key_rows, value_rows, attn_out, grad_out, log_norms, pair_order):
    def heads_first(rows):
        return jnp.transpose(rows, (1, 0, 2))

    half = jnp.bfloat16
    full = jnp.float32
    dma = pltpu.SemaphoreType.DMA
    vmem = pl.BlockSpec(memory_space=pltpu.VMEM)
    hbm = pl.BlockSpec(memory_space=pltpu.HBM)
    grads = (
        jax.ShapeDtypeStruct((HEADS, ROWS, DIM), half),
        jax.ShapeDtypeStruct((ROWS, DIM), half),
        jax.ShapeDtypeStruct((ROWS, DIM), half),
    )
    parts = pl.pallas_call(
        kernel,
        out_shape=grads,
        in_specs=[pl.BlockSpec(memory_space=pltpu.SMEM), hbm, hbm, hbm, hbm, hbm, hbm],
        out_specs=(hbm, hbm, hbm),
        scratch_shapes=[
            pltpu.VMEM((Y_DEVICES, 2, GROUP_KEYS, DIM), half),
            pltpu.VMEM((2, HEADS, ROWS, DIM), half),
            pltpu.VMEM((2, HEADS, ROWS, DIM), half),
            pltpu.VMEM((HEADS, ROWS, DIM), half),
            pltpu.VMEM((HEADS, ROWS), full),
            pltpu.VMEM((2, 2, 8, ROWS), full),
            pltpu.VMEM((Y_DEVICES, GROUP_KEYS, DIM), jnp.int32),
            pltpu.VMEM((GROUP_KEYS, HEADS * ROWS), half),
            pltpu.VMEM((Y_DEVICES, GROUP_KEYS, HEADS * ROWS), half),
            pltpu.VMEM((Y_DEVICES, GROUP_KEYS, HEADS * ROWS), half),
            pltpu.VMEM((Y_DEVICES, 2, GROUP_KEYS, DIM), full),
            pltpu.VMEM((HEADS * ROWS, DIM), full),
            pltpu.VMEM((Y_DEVICES, 2, GROUP_KEYS, DIM), half),
            pltpu.VMEM((Y_DEVICES, 3, 2, ROWS, DIM), half),
            pltpu.VMEM((3, 2, ROWS, DIM), half),
            pltpu.VMEM((3, 2, ROWS, DIM), half),
            pltpu.VMEM((HEADS * ROWS, DIM), half),
            pltpu.VMEM((HEADS * ROWS, DIM), half),
            pltpu.VMEM((HEADS, ROWS, DIM), half),
            pltpu.VMEM((2, ROWS, DIM), half),
            dma((6,)), dma((3,)), dma((3,)), dma((3, 2)), dma((3, 2)), dma((3, 3, 2)),
            dma((16, 2)), dma((4, 3, 2)), dma((4, 3, 2)), dma((3, 2)), dma((3, 2)), dma, dma,
        ],
        compiler_params=pltpu.CompilerParams(
            collective_id=0, has_side_effects=True, vmem_limit_bytes=60 * 2**20
        ),
        cost_estimate=pl.CostEstimate(
            flops=4 * 10**9, bytes_accessed=10**6, transcendentals=3 * 10**6
        ),
    )(
        pair_order,
        heads_first(queries),
        key_rows.reshape(ROWS, DIM),
        value_rows.reshape(ROWS, DIM),
        heads_first(attn_out),
        heads_first(grad_out),
        log_norms,
    )
    grad_queries, grad_keys, grad_values = pl.pallas_call(
        store_kernel,
        out_shape=grads,
        in_specs=[vmem, vmem, vmem],
        out_specs=(hbm, hbm, hbm),
        scratch_shapes=[dma((3,))],
    )(*parts)
    return (
        jnp.transpose(grad_queries, (1, 0, 2)),
        grad_keys.reshape(ROWS, 1, DIM),
        grad_values.reshape(ROWS, 1, DIM),
    )


def solution(mesh):
    rows = P(("outer", "inner"), "head", None)
    return jax.shard_map(
        on_device,
        mesh=mesh,
        in_specs=(rows, rows, rows, rows, rows, P("head", ("outer", "inner")), P()),
        out_specs=(rows, rows, rows),
        check_vma=False,
    )
```

```python
import functools
import math

import jax
import jax.numpy as jnp
from jax import lax
from jax.experimental import pallas as pl
from jax.experimental.pallas import tpu as pltpu
from jax.sharding import PartitionSpec as P

MESH = pl.DeviceIdType.MESH
LOG2E = math.log2(math.e)
X_DEVICES = 4
Y_DEVICES = 4
ROWS = 128
HEADS = 6
DIM = 128
SPAN = 64
GROUP_KEYS = Y_DEVICES * ROWS
PAIRS = HEADS // 2
OUTER = 8

NT = (((1,), (1,)), ((), ()))
TN = (((0,), (0,)), ((), ()))
NN = (((1,), (0,)), ((), ()))


def dot(a, b, dims):
    return lax.dot_general(a, b, dims, preferred_element_type=jnp.float32)


def kernel(
    order_ref, q_ref, k_ref, v_ref, o_ref, g_ref, lse_ref,
    dq_ref, dk_ref, dv_ref,
    kv, qs, gs, attn, lse, stat, kpos, weights, own_scores, next_scores, acc, dq_next,
    sx, rx, sy, ry, sq, rq,
    local_sem, z_send, z_recv, ag_send_y, ag_send_own, ag_send_x, ag_recv,
    rs_send_x, rs_recv_x, rs_send_y, rs_recv_y, dq_send, dq_recv,
):
    inner = lax.axis_index("inner")
    outer = lax.axis_index("outer")
    head = lax.axis_index("head")
    x = inner // Y_DEVICES
    y = lax.rem(inner, Y_DEVICES)
    inv_root = 1.0 / math.sqrt(DIM)

    def at_x(distance):
        return (lax.rem(x + distance, X_DEVICES) * Y_DEVICES + y, outer, head)

    def at_y(distance):
        return (x * Y_DEVICES + lax.rem(y + distance, Y_DEVICES), outer, head)

    def at_z(distance):
        return (inner, outer + distance, head)

    def rows_of(xi):
        return pl.ds(pl.multiple_of(xi * ROWS, ROWS), ROWS)

    def block(xi, yi, i):
        return kv.at[yi, i, rows_of(xi), :]

    loads = [
        pltpu.make_async_copy(k_ref, kv.at[y, 0, rows_of(x), :], local_sem.at[0]),
        pltpu.make_async_copy(v_ref, kv.at[y, 1, rows_of(x), :], local_sem.at[1]),
        pltpu.make_async_copy(g_ref, gs.at[0], local_sem.at[2]),
        pltpu.make_async_copy(o_ref, attn, local_sem.at[3]),
        pltpu.make_async_copy(lse_ref, lse, local_sem.at[4]),
        pltpu.make_async_copy(q_ref, qs.at[0], local_sem.at[5]),
    ]
    for load in loads:
        load.start()

    barrier = pltpu.get_barrier_semaphore()
    for distance in (1, 2, 3):
        pl.semaphore_signal(barrier, inc=1, device_id=at_x(distance), device_id_type=MESH)
        pl.semaphore_signal(barrier, inc=1, device_id=at_y(distance), device_id_type=MESH)

    @pl.when(outer > 0)
    def _():
        pl.semaphore_signal(barrier, inc=1, device_id=at_z(-1), device_id_type=MESH)

    @pl.when(outer < OUTER - 1)
    def _():
        pl.semaphore_signal(barrier, inc=1, device_id=at_z(1), device_id_type=MESH)

    peers = 6 + jnp.minimum(outer, 1) + jnp.minimum(OUTER - 1 - outer, 1)
    pl.semaphore_wait(barrier, peers)

    def send_own(i, target, sems, slot):
        return pltpu.make_async_remote_copy(
            (k_ref, v_ref)[i], block(x, y, i), sems.at[slot, i],
            ag_recv.at[x * Y_DEVICES + y, i], device_id=target, device_id_type=MESH,
        )

    def send_y(distance, i):
        return send_own(i, at_y(distance), ag_send_y, distance - 1)

    def send_x(step, distance, i):
        if step == 0:
            return send_own(i, at_x(distance), ag_send_own, distance - 1)
        yi = lax.rem(y + step, Y_DEVICES)
        return pltpu.make_async_remote_copy(
            block(x, yi, i), block(x, yi, i), ag_send_x.at[step - 1, distance - 1, i],
            ag_recv.at[x * Y_DEVICES + yi, i], device_id=at_x(distance), device_id_type=MESH,
        )

    def wait_block(xi, yi, i):
        pltpu.make_async_remote_copy(
            block(xi, yi, i), block(xi, yi, i), ag_send_y.at[0, 0],
            ag_recv.at[xi * Y_DEVICES + yi, i], device_id=at_y(1), device_id_type=MESH,
        ).wait_recv()

    def z_copies():
        return [
            pltpu.make_async_remote_copy(
                source, landing.at[1], z_send.at[i], z_recv.at[i],
                device_id=at_z(-1), device_id_type=MESH,
            )
            for i, (source, landing) in enumerate(((q_ref, qs), (g_ref, gs), (stat.at[0], stat)))
        ]

    @pl.when(outer > 0)
    def _():
        for copy in z_copies()[:2]:
            copy.start()

    for i in (0, 1):
        for distance in (1, 3, 2):
            send_y(distance, i).start()

    for i in (0, 1):
        for distance in (1, 3, 2):
            send_x(0, distance, i).start()

    for load in loads:
        load.wait()

    stat[0, 0, 0:HEADS, :] = lse[...] * LOG2E
    ones = jnp.ones((8, DIM), jnp.bfloat16)
    for h in range(HEADS):
        product = gs[0, h].astype(jnp.float32) * attn[h].astype(jnp.float32)
        high = product.astype(jnp.bfloat16)
        low = (product - high.astype(jnp.float32)).astype(jnp.bfloat16)
        sums = dot(ones, high, NT) + dot(ones, low, NT)
        stat[0, 1, h : h + 1, :] = sums[0:1, :]

    row = lax.broadcasted_iota(jnp.int32, (SPAN, DIM), 0)
    for device in range(X_DEVICES * Y_DEVICES):
        rank = order_ref[device]
        xi, yi = divmod(device, Y_DEVICES)
        kpos[yi, xi * ROWS : xi * ROWS + SPAN, :] = row + rank * SPAN
        kpos[yi, xi * ROWS + SPAN : (xi + 1) * ROWS, :] = (
            row + (2 * X_DEVICES * Y_DEVICES - 1 - rank) * SPAN
        )
    lane = lax.broadcasted_iota(jnp.int32, (1, ROWS), 1)
    rank = order_ref[inner]
    qpos = jnp.where(
        lane < SPAN,
        rank * SPAN + lane,
        (2 * X_DEVICES * Y_DEVICES - 1 - rank) * SPAN + lane - SPAN,
    )
    qpos = jnp.concatenate([qpos, qpos], axis=1)

    @pl.when(outer > 0)
    def _():
        z_copies()[2].start()

    def tile(step, half, scores):
        yi = lax.rem(y + step, Y_DEVICES)
        keys = kv[yi, 0]
        values = kv[yi, 1]
        if half == 0:
            column = kpos[yi]
            column = jnp.concatenate([column, column], axis=1)
        for pair in range(PAIRS):
            two = slice(2 * pair, 2 * pair + 2)
            q_two = qs[half, two].reshape(2 * ROWS, DIM)
            g_two = gs[half, two].reshape(2 * ROWS, DIM)
            norms = jnp.concatenate(
                [stat[half, 0, 2 * pair + i : 2 * pair + i + 1, :] for i in (0, 1)], axis=1
            )
            dots = jnp.concatenate(
                [stat[half, 1, 2 * pair + i : 2 * pair + i + 1, :] for i in (0, 1)], axis=1
            )
            p = jnp.exp2(dot(keys, q_two, NT) * (inv_root * LOG2E) - norms)
            if half == 0:
                p = jnp.where(column <= qpos, p, 0.0)
            lanes = slice(2 * pair * ROWS, 2 * (pair + 1) * ROWS)
            weights[:, lanes] = p.astype(jnp.bfloat16)
            ds = (p * (dot(values, g_two, NT) - dots)).astype(jnp.bfloat16)
            scores[step, :, lanes] = ds

    def key_grad(step, half, i):
        if i == 0:
            scores = (own_scores, next_scores)[half]
            return dot(scores[step], qs[half].reshape(HEADS * ROWS, DIM), NN)
        return dot(weights[...], gs[half].reshape(HEADS * ROWS, DIM), NN)

    def own_tile(step):
        tile(step, 0, own_scores)
        for i in (0, 1):
            acc[step, i] = key_grad(step, 0, i)

    def query_grads(scores, steps):
        total = None
        for step in steps:
            part = dot(scores[step], kv[lax.rem(y + step, Y_DEVICES), 0], TN)
            total = part if total is None else total + part
        return total

    def pass_on(step):
        for i in (0, 1):
            wait_block(x, lax.rem(y + step, Y_DEVICES), i)
            for distance in (1, 3, 2):
                send_x(step, distance, i).start()

    def wait_others(step):
        for i in (0, 1):
            for distance in (1, 3, 2):
                wait_block(lax.rem(x + distance, X_DEVICES), lax.rem(y + step, Y_DEVICES), i)

    def rs_x(step, distance, i):
        xi = lax.rem(x + distance, X_DEVICES)
        return pltpu.make_async_remote_copy(
            sx.at[step, i, rows_of(xi), :], rx.at[step, distance - 1, i],
            rs_send_x.at[step, distance - 1, i], rs_recv_x.at[step, distance - 1, i],
            device_id=at_x(distance), device_id_type=MESH,
        )

    def rs_y(step, i):
        return pltpu.make_async_remote_copy(
            sy.at[step - 1, i], ry.at[step - 1, i], rs_send_y.at[step - 1, i],
            rs_recv_y.at[step - 1, i], device_id=at_y(step), device_id_type=MESH,
        )

    def next_tile(step):
        tile(step, 1, next_scores)
        for i in (0, 1):
            grad = acc[step, i] + key_grad(step, 1, i)
            if i == 0:
                grad = grad * inv_root
            acc[step, i] = grad
            sx[step, i] = grad.astype(jnp.bfloat16)
            for distance in (2, 1, 3):
                rs_x(step, distance, i).start()

    def over_x(step, i):
        total = acc[step, i, rows_of(x), :]
        for distance in (1, 2, 3):
            rs_x(step, distance, i).wait_recv()
            total = total + rx[step, distance - 1, i].astype(jnp.float32)
        return total

    def to_y(step):
        for i in (0, 1):
            sy[step - 1, i] = over_x(step, i).astype(jnp.bfloat16)
            rs_y(step, i).start()

    def dq_copy(distance):
        return pltpu.make_async_remote_copy(
            sq, rq, dq_send, dq_recv, device_id=at_z(distance), device_id_type=MESH
        )

    pass_on(1)
    pass_on(3)
    wait_others(0)
    own_tile(0)
    pass_on(2)
    wait_others(1)
    own_tile(1)

    @pl.when(outer < OUTER - 1)
    def _():
        for copy in z_copies():
            copy.wait_recv()

    @pl.when(outer == OUTER - 1)
    def _():
        stat[1] = jnp.zeros_like(stat[1])
        qs[1] = jnp.zeros_like(qs[1])
        gs[1] = jnp.zeros_like(gs[1])

    next_tile(1)
    wait_others(3)
    own_tile(3)
    wait_others(2)
    own_tile(2)
    next_tile(2)
    next_tile(3)
    to_y(1)
    dq_next[...] = query_grads(next_scores, (2, 1, 3))
    next_tile(0)
    sq[...] = (
        (dq_next[...] + query_grads(next_scores, (0,))) * inv_root
    ).astype(jnp.bfloat16)

    @pl.when(outer < OUTER - 1)
    def _():
        dq_copy(1).start()

    to_y(2)
    to_y(3)
    totals = [over_x(0, 0), over_x(0, 1)]
    own = query_grads(own_scores, range(Y_DEVICES)) * inv_root

    @pl.when(outer > 0)
    def _():
        dq_copy(-1).wait_recv()

    @pl.when(outer == 0)
    def _():
        rq[...] = jnp.zeros_like(rq)

    dq_ref[...] = (
        (own + rq[...].astype(jnp.float32)).astype(jnp.bfloat16).reshape(HEADS, ROWS, DIM)
    )

    for i in (0, 1):
        total = totals[i]
        for step in (1, 3, 2):
            rs_y(step, i).wait_recv()
            total = total + ry[step - 1, i].astype(jnp.float32)
        (dk_ref, dv_ref)[i][...] = total.astype(jnp.bfloat16)

    for i in (0, 1):
        for distance in (1, 2, 3):
            send_y(distance, i).wait_send()
            rs_y(distance, i).wait_send()
            for step in range(Y_DEVICES):
                send_x(step, distance, i).wait_send()
                rs_x(step, distance, i).wait_send()

    @pl.when(outer > 0)
    def _():
        for copy in z_copies():
            copy.wait_send()

    @pl.when(outer < OUTER - 1)
    def _():
        dq_copy(1).wait_send()


def store_kernel(dq_in, dk_in, dv_in, dq_ref, dk_ref, dv_ref, sems):
    copies = [
        pltpu.make_async_copy(dq_in, dq_ref, sems.at[0]),
        pltpu.make_async_copy(dk_in, dk_ref, sems.at[1]),
        pltpu.make_async_copy(dv_in, dv_ref, sems.at[2]),
    ]
    for copy in copies:
        copy.start()
    for copy in copies:
        copy.wait()


def on_device(queries, key_rows, value_rows, attn_out, grad_out, log_norms, pair_order):
    def heads_first(rows):
        return jnp.transpose(rows, (1, 0, 2))

    half = jnp.bfloat16
    full = jnp.float32
    dma = pltpu.SemaphoreType.DMA
    vmem = pl.BlockSpec(memory_space=pltpu.VMEM)
    hbm = pl.BlockSpec(memory_space=pltpu.HBM)
    grads = (
        jax.ShapeDtypeStruct((HEADS, ROWS, DIM), half),
        jax.ShapeDtypeStruct((ROWS, DIM), half),
        jax.ShapeDtypeStruct((ROWS, DIM), half),
    )
    parts = pl.pallas_call(
        kernel,
        out_shape=tuple(pltpu.VMEM(grad.shape, grad.dtype) for grad in grads),
        in_specs=[pl.BlockSpec(memory_space=pltpu.SMEM), hbm, hbm, hbm, hbm, hbm, hbm],
        out_specs=(vmem, vmem, vmem),
        scratch_shapes=[
            pltpu.VMEM((Y_DEVICES, 2, GROUP_KEYS, DIM), half),
            pltpu.VMEM((2, HEADS, ROWS, DIM), half),
            pltpu.VMEM((2, HEADS, ROWS, DIM), half),
            pltpu.VMEM((HEADS, ROWS, DIM), half),
            pltpu.VMEM((HEADS, ROWS), full),
            pltpu.VMEM((2, 2, 8, ROWS), full),
            pltpu.VMEM((Y_DEVICES, GROUP_KEYS, DIM), jnp.int32),
            pltpu.VMEM((GROUP_KEYS, HEADS * ROWS), half),
            pltpu.VMEM((Y_DEVICES, GROUP_KEYS, HEADS * ROWS), half),
            pltpu.VMEM((Y_DEVICES, GROUP_KEYS, HEADS * ROWS), half),
            pltpu.VMEM((Y_DEVICES, 2, GROUP_KEYS, DIM), full),
            pltpu.VMEM((HEADS * ROWS, DIM), full),
            pltpu.VMEM((Y_DEVICES, 2, GROUP_KEYS, DIM), half),
            pltpu.VMEM((Y_DEVICES, 3, 2, ROWS, DIM), half),
            pltpu.VMEM((3, 2, ROWS, DIM), half),
            pltpu.VMEM((3, 2, ROWS, DIM), half),
            pltpu.VMEM((HEADS * ROWS, DIM), half),
            pltpu.VMEM((HEADS * ROWS, DIM), half),
            dma((6,)), dma((3,)), dma((3,)), dma((3, 2)), dma((3, 2)), dma((3, 3, 2)),
            dma((16, 2)), dma((4, 3, 2)), dma((4, 3, 2)), dma((3, 2)), dma((3, 2)), dma, dma,
        ],
        compiler_params=pltpu.CompilerParams(
            collective_id=0, has_side_effects=True, vmem_limit_bytes=60 * 2**20
        ),
        cost_estimate=pl.CostEstimate(
            flops=4 * 10**9, bytes_accessed=10**6, transcendentals=3 * 10**6
        ),
    )(
        pair_order,
        heads_first(queries),
        key_rows.reshape(ROWS, DIM),
        value_rows.reshape(ROWS, DIM),
        heads_first(attn_out),
        heads_first(grad_out),
        log_norms,
    )
    grad_queries, grad_keys, grad_values = pl.pallas_call(
        store_kernel,
        out_shape=grads,
        in_specs=[vmem, vmem, vmem],
        out_specs=(hbm, hbm, hbm),
        scratch_shapes=[dma((3,))],
        compiler_params=pltpu.CompilerParams(vmem_limit_bytes=2**20),
    )(*parts)
    return (
        jnp.transpose(grad_queries, (1, 0, 2)),
        grad_keys.reshape(ROWS, 1, DIM),
        grad_values.reshape(ROWS, 1, DIM),
    )


def solution(mesh):
    rows = P(("outer", "inner"), "head", None)
    return jax.shard_map(
        on_device,
        mesh=mesh,
        in_specs=(rows, rows, rows, rows, rows, P("head", ("outer", "inner")), P()),
        out_specs=(rows, rows, rows),
        check_vma=False,
    )
```

```python
import functools
import math

import jax
import jax.numpy as jnp
from jax import lax
from jax.experimental import pallas as pl
from jax.experimental.pallas import tpu as pltpu
from jax.sharding import PartitionSpec as P

MESH = pl.DeviceIdType.MESH
LOG2E = math.log2(math.e)
X_DEVICES = 4
Y_DEVICES = 4
ROWS = 128
HEADS = 6
DIM = 128
SPAN = 64
GROUP_KEYS = Y_DEVICES * ROWS
PAIRS = HEADS // 2
OUTER = 8

NT = (((1,), (1,)), ((), ()))
TN = (((0,), (0,)), ((), ()))
NN = (((1,), (0,)), ((), ()))


def dot(a, b, dims):
    return lax.dot_general(a, b, dims, preferred_element_type=jnp.float32)


def kernel(
    order_ref, q_ref, k_ref, v_ref, o_ref, g_ref, lse_ref,
    dq_ref, dk_ref, dv_ref,
    kv, qs, gs, attn, lse, stat, kpos, weights, own_scores, next_scores, acc, dq_next,
    sx, rx, sy, ry, sq, rq,
    local_sem, z_send, z_recv, ag_send_y, ag_send_own, ag_send_x, ag_recv,
    rs_send_x, rs_recv_x, rs_send_y, rs_recv_y, dq_send, dq_recv,
):
    inner = lax.axis_index("inner")
    outer = lax.axis_index("outer")
    head = lax.axis_index("head")
    x = inner // Y_DEVICES
    y = lax.rem(inner, Y_DEVICES)
    inv_root = 1.0 / math.sqrt(DIM)

    def at_x(distance):
        return (lax.rem(x + distance, X_DEVICES) * Y_DEVICES + y, outer, head)

    def at_y(distance):
        return (x * Y_DEVICES + lax.rem(y + distance, Y_DEVICES), outer, head)

    def at_z(distance):
        return (inner, outer + distance, head)

    def rows_of(xi):
        return pl.ds(pl.multiple_of(xi * ROWS, ROWS), ROWS)

    def block(xi, yi, i):
        return kv.at[yi, i, rows_of(xi), :]

    barrier = pltpu.get_barrier_semaphore()
    for distance in (1, 2, 3):
        pl.semaphore_signal(barrier, inc=1, device_id=at_x(distance), device_id_type=MESH)
        pl.semaphore_signal(barrier, inc=1, device_id=at_y(distance), device_id_type=MESH)

    @pl.when(outer > 0)
    def _():
        pl.semaphore_signal(barrier, inc=1, device_id=at_z(-1), device_id_type=MESH)

    @pl.when(outer < OUTER - 1)
    def _():
        pl.semaphore_signal(barrier, inc=1, device_id=at_z(1), device_id_type=MESH)

    loads = [
        pltpu.make_async_copy(k_ref, kv.at[y, 0, rows_of(x), :], local_sem.at[0]),
        pltpu.make_async_copy(v_ref, kv.at[y, 1, rows_of(x), :], local_sem.at[1]),
        pltpu.make_async_copy(g_ref, gs.at[0], local_sem.at[2]),
        pltpu.make_async_copy(o_ref, attn, local_sem.at[3]),
        pltpu.make_async_copy(lse_ref, lse, local_sem.at[4]),
        pltpu.make_async_copy(q_ref, qs.at[0], local_sem.at[5]),
    ]
    for load in loads:
        load.start()

    peers = 6 + jnp.minimum(outer, 1) + jnp.minimum(OUTER - 1 - outer, 1)
    pl.semaphore_wait(barrier, peers)

    def send_own(i, target, sems, slot):
        return pltpu.make_async_remote_copy(
            (k_ref, v_ref)[i], block(x, y, i), sems.at[slot, i],
            ag_recv.at[x * Y_DEVICES + y, i], device_id=target, device_id_type=MESH,
        )

    def send_y(distance, i):
        return send_own(i, at_y(distance), ag_send_y, distance - 1)

    def send_x(step, distance, i):
        if step == 0:
            return send_own(i, at_x(distance), ag_send_own, distance - 1)
        yi = lax.rem(y + step, Y_DEVICES)
        return pltpu.make_async_remote_copy(
            block(x, yi, i), block(x, yi, i), ag_send_x.at[step - 1, distance - 1, i],
            ag_recv.at[x * Y_DEVICES + yi, i], device_id=at_x(distance), device_id_type=MESH,
        )

    def wait_block(xi, yi, i):
        pltpu.make_async_remote_copy(
            block(xi, yi, i), block(xi, yi, i), ag_send_y.at[0, 0],
            ag_recv.at[xi * Y_DEVICES + yi, i], device_id=at_y(1), device_id_type=MESH,
        ).wait_recv()

    def z_copies():
        return [
            pltpu.make_async_remote_copy(
                source, landing.at[1], z_send.at[i], z_recv.at[i],
                device_id=at_z(-1), device_id_type=MESH,
            )
            for i, (source, landing) in enumerate(((q_ref, qs), (g_ref, gs), (stat.at[0], stat)))
        ]

    @pl.when(outer > 0)
    def _():
        for copy in z_copies()[:2]:
            copy.start()

    for distance in (1, 3, 2):
        for i in (0, 1):
            send_y(distance, i).start()

    for i in (0, 1):
        for distance in (1, 3, 2):
            send_x(0, distance, i).start()

    for load in loads:
        load.wait()

    stat[0, 0, 0:HEADS, :] = lse[...] * LOG2E
    ones = jnp.ones((8, DIM), jnp.bfloat16)
    for h in range(HEADS):
        product = gs[0, h].astype(jnp.float32) * attn[h].astype(jnp.float32)
        high = product.astype(jnp.bfloat16)
        low = (product - high.astype(jnp.float32)).astype(jnp.bfloat16)
        sums = dot(ones, high, NT) + dot(ones, low, NT)
        stat[0, 1, h : h + 1, :] = sums[0:1, :]

    row = lax.broadcasted_iota(jnp.int32, (SPAN, DIM), 0)
    for device in range(X_DEVICES * Y_DEVICES):
        rank = order_ref[device]
        xi, yi = divmod(device, Y_DEVICES)
        kpos[yi, xi * ROWS : xi * ROWS + SPAN, :] = row + rank * SPAN
        kpos[yi, xi * ROWS + SPAN : (xi + 1) * ROWS, :] = (
            row + (2 * X_DEVICES * Y_DEVICES - 1 - rank) * SPAN
        )
    lane = lax.broadcasted_iota(jnp.int32, (1, ROWS), 1)
    rank = order_ref[inner]
    qpos = jnp.where(
        lane < SPAN,
        rank * SPAN + lane,
        (2 * X_DEVICES * Y_DEVICES - 1 - rank) * SPAN + lane - SPAN,
    )
    qpos = jnp.concatenate([qpos, qpos], axis=1)

    @pl.when(outer > 0)
    def _():
        z_copies()[2].start()

    def tile(step, half, scores):
        yi = lax.rem(y + step, Y_DEVICES)
        keys = kv[yi, 0]
        values = kv[yi, 1]
        if half == 0:
            column = kpos[yi]
            column = jnp.concatenate([column, column], axis=1)
        for pair in range(PAIRS):
            two = slice(2 * pair, 2 * pair + 2)
            q_two = qs[half, two].reshape(2 * ROWS, DIM)
            g_two = gs[half, two].reshape(2 * ROWS, DIM)
            norms = jnp.concatenate(
                [stat[half, 0, 2 * pair + i : 2 * pair + i + 1, :] for i in (0, 1)], axis=1
            )
            dots = jnp.concatenate(
                [stat[half, 1, 2 * pair + i : 2 * pair + i + 1, :] for i in (0, 1)], axis=1
            )
            p = jnp.exp2(dot(keys, q_two, NT) * (inv_root * LOG2E) - norms)
            if half == 0:
                p = jnp.where(column <= qpos, p, 0.0)
            lanes = slice(2 * pair * ROWS, 2 * (pair + 1) * ROWS)
            weights[:, lanes] = p.astype(jnp.bfloat16)
            ds = (p * (dot(values, g_two, NT) - dots)).astype(jnp.bfloat16)
            scores[step, :, lanes] = ds

    def key_grad(step, half, i):
        if i == 0:
            scores = (own_scores, next_scores)[half]
            return dot(scores[step], qs[half].reshape(HEADS * ROWS, DIM), NN)
        return dot(weights[...], gs[half].reshape(HEADS * ROWS, DIM), NN)

    def own_tile(step):
        tile(step, 0, own_scores)
        for i in (0, 1):
            acc[step, i] = key_grad(step, 0, i)

    def query_grads(scores, steps):
        total = None
        for step in steps:
            part = dot(scores[step], kv[lax.rem(y + step, Y_DEVICES), 0], TN)
            total = part if total is None else total + part
        return total

    def pass_on(step):
        for i in (0, 1):
            wait_block(x, lax.rem(y + step, Y_DEVICES), i)
            for distance in (1, 3, 2):
                send_x(step, distance, i).start()

    def wait_others(step):
        for i in (0, 1):
            for distance in (1, 3, 2):
                wait_block(lax.rem(x + distance, X_DEVICES), lax.rem(y + step, Y_DEVICES), i)

    def rs_x(step, distance, i):
        xi = lax.rem(x + distance, X_DEVICES)
        return pltpu.make_async_remote_copy(
            sx.at[step, i, rows_of(xi), :], rx.at[step, distance - 1, i],
            rs_send_x.at[step, distance - 1, i], rs_recv_x.at[step, distance - 1, i],
            device_id=at_x(distance), device_id_type=MESH,
        )

    def rs_y(step, i):
        return pltpu.make_async_remote_copy(
            sy.at[step - 1, i], ry.at[step - 1, i], rs_send_y.at[step - 1, i],
            rs_recv_y.at[step - 1, i], device_id=at_y(step), device_id_type=MESH,
        )

    def send_tile(step):
        for i in (0, 1):
            for distance in (2, 1, 3):
                rs_x(step, distance, i).start()

    def next_tile(step, send=True):
        tile(step, 1, next_scores)
        for i in (0, 1):
            grad = acc[step, i] + key_grad(step, 1, i)
            if i == 0:
                grad = grad * inv_root
            acc[step, i] = grad
            sx[step, i] = grad.astype(jnp.bfloat16)
            if send:
                for distance in (2, 1, 3):
                    rs_x(step, distance, i).start()

    def over_x(step, i):
        total = acc[step, i, rows_of(x), :]
        for distance in (1, 2, 3):
            rs_x(step, distance, i).wait_recv()
            total = total + rx[step, distance - 1, i].astype(jnp.float32)
        return total

    def to_y(step):
        for i in (0, 1):
            sy[step - 1, i] = over_x(step, i).astype(jnp.bfloat16)
            rs_y(step, i).start()

    def dq_copy(distance):
        return pltpu.make_async_remote_copy(
            sq, rq, dq_send, dq_recv, device_id=at_z(distance), device_id_type=MESH
        )

    pass_on(1)
    pass_on(3)
    wait_others(0)
    own_tile(0)
    pass_on(2)
    wait_others(1)
    own_tile(1)

    @pl.when(outer < OUTER - 1)
    def _():
        for copy in z_copies():
            copy.wait_recv()

    @pl.when(outer == OUTER - 1)
    def _():
        stat[1] = jnp.zeros_like(stat[1])
        qs[1] = jnp.zeros_like(qs[1])
        gs[1] = jnp.zeros_like(gs[1])

    next_tile(1)
    wait_others(3)
    own_tile(3)
    next_tile(3, False)
    wait_others(2)
    own_tile(2)
    next_tile(2)
    send_tile(3)
    to_y(1)
    dq_next[...] = query_grads(next_scores, (2, 1, 3))
    next_tile(0)
    sq[...] = (
        (dq_next[...] + query_grads(next_scores, (0,))) * inv_root
    ).astype(jnp.bfloat16)

    @pl.when(outer < OUTER - 1)
    def _():
        dq_copy(1).start()

    to_y(2)
    to_y(3)
    totals = [over_x(0, 0), over_x(0, 1)]
    own = query_grads(own_scores, range(Y_DEVICES)) * inv_root

    @pl.when(outer > 0)
    def _():
        dq_copy(-1).wait_recv()

    @pl.when(outer == 0)
    def _():
        rq[...] = jnp.zeros_like(rq)

    dq_ref[...] = (
        (own + rq[...].astype(jnp.float32)).astype(jnp.bfloat16).reshape(HEADS, ROWS, DIM)
    )

    for i in (0, 1):
        total = totals[i]
        for step in (1, 3, 2):
            rs_y(step, i).wait_recv()
            total = total + ry[step - 1, i].astype(jnp.float32)
        (dk_ref, dv_ref)[i][...] = total.astype(jnp.bfloat16)

    for i in (0, 1):
        for distance in (1, 2, 3):
            send_y(distance, i).wait_send()
            rs_y(distance, i).wait_send()
            for step in range(Y_DEVICES):
                send_x(step, distance, i).wait_send()
                rs_x(step, distance, i).wait_send()

    @pl.when(outer > 0)
    def _():
        for copy in z_copies():
            copy.wait_send()

    @pl.when(outer < OUTER - 1)
    def _():
        dq_copy(1).wait_send()


def store_kernel(dq_in, dk_in, dv_in, dq_ref, dk_ref, dv_ref, sems):
    copies = [
        pltpu.make_async_copy(dq_in, dq_ref, sems.at[0]),
        pltpu.make_async_copy(dk_in, dk_ref, sems.at[1]),
        pltpu.make_async_copy(dv_in, dv_ref, sems.at[2]),
    ]
    for copy in copies:
        copy.start()
    for copy in copies:
        copy.wait()


def on_device(queries, key_rows, value_rows, attn_out, grad_out, log_norms, pair_order):
    def heads_first(rows):
        return jnp.transpose(rows, (1, 0, 2))

    half = jnp.bfloat16
    full = jnp.float32
    dma = pltpu.SemaphoreType.DMA
    vmem = pl.BlockSpec(memory_space=pltpu.VMEM)
    hbm = pl.BlockSpec(memory_space=pltpu.HBM)
    grads = (
        jax.ShapeDtypeStruct((HEADS, ROWS, DIM), half),
        jax.ShapeDtypeStruct((ROWS, DIM), half),
        jax.ShapeDtypeStruct((ROWS, DIM), half),
    )
    parts = pl.pallas_call(
        kernel,
        out_shape=tuple(pltpu.VMEM(grad.shape, grad.dtype) for grad in grads),
        in_specs=[pl.BlockSpec(memory_space=pltpu.SMEM), hbm, hbm, hbm, hbm, hbm, hbm],
        out_specs=(vmem, vmem, vmem),
        scratch_shapes=[
            pltpu.VMEM((Y_DEVICES, 2, GROUP_KEYS, DIM), half),
            pltpu.VMEM((2, HEADS, ROWS, DIM), half),
            pltpu.VMEM((2, HEADS, ROWS, DIM), half),
            pltpu.VMEM((HEADS, ROWS, DIM), half),
            pltpu.VMEM((HEADS, ROWS), full),
            pltpu.VMEM((2, 2, 8, ROWS), full),
            pltpu.VMEM((Y_DEVICES, GROUP_KEYS, DIM), jnp.int32),
            pltpu.VMEM((GROUP_KEYS, HEADS * ROWS), half),
            pltpu.VMEM((Y_DEVICES, GROUP_KEYS, HEADS * ROWS), half),
            pltpu.VMEM((Y_DEVICES, GROUP_KEYS, HEADS * ROWS), half),
            pltpu.VMEM((Y_DEVICES, 2, GROUP_KEYS, DIM), full),
            pltpu.VMEM((HEADS * ROWS, DIM), full),
            pltpu.VMEM((Y_DEVICES, 2, GROUP_KEYS, DIM), half),
            pltpu.VMEM((Y_DEVICES, 3, 2, ROWS, DIM), half),
            pltpu.VMEM((3, 2, ROWS, DIM), half),
            pltpu.VMEM((3, 2, ROWS, DIM), half),
            pltpu.VMEM((HEADS * ROWS, DIM), half),
            pltpu.VMEM((HEADS * ROWS, DIM), half),
            dma((6,)), dma((3,)), dma((3,)), dma((3, 2)), dma((3, 2)), dma((3, 3, 2)),
            dma((16, 2)), dma((4, 3, 2)), dma((4, 3, 2)), dma((3, 2)), dma((3, 2)), dma, dma,
        ],
        compiler_params=pltpu.CompilerParams(
            collective_id=0, has_side_effects=True, vmem_limit_bytes=60 * 2**20
        ),
        cost_estimate=pl.CostEstimate(
            flops=4 * 10**9, bytes_accessed=10**6, transcendentals=3 * 10**6
        ),
    )(
        pair_order,
        heads_first(queries),
        key_rows.reshape(ROWS, DIM),
        value_rows.reshape(ROWS, DIM),
        heads_first(attn_out),
        heads_first(grad_out),
        log_norms,
    )
    grad_queries, grad_keys, grad_values = pl.pallas_call(
        store_kernel,
        out_shape=grads,
        in_specs=[vmem, vmem, vmem],
        out_specs=(hbm, hbm, hbm),
        scratch_shapes=[dma((3,))],
        compiler_params=pltpu.CompilerParams(vmem_limit_bytes=2**20),
    )(*parts)
    return (
        jnp.transpose(grad_queries, (1, 0, 2)),
        grad_keys.reshape(ROWS, 1, DIM),
        grad_values.reshape(ROWS, 1, DIM),
    )


def solution(mesh):
    rows = P(("outer", "inner"), "head", None)
    return jax.shard_map(
        on_device,
        mesh=mesh,
        in_specs=(rows, rows, rows, rows, rows, P("head", ("outer", "inner")), P()),
        out_specs=(rows, rows, rows),
        check_vma=False,
    )
```

```python
import functools
import math

import jax
import jax.numpy as jnp
from jax import lax
from jax.experimental import pallas as pl
from jax.experimental.pallas import tpu as pltpu
from jax.sharding import PartitionSpec as P

MESH = pl.DeviceIdType.MESH
LOG2E = math.log2(math.e)
X_DEVICES = 4
Y_DEVICES = 4
ROWS = 128
HEADS = 6
DIM = 128
SPAN = 64
GROUP_KEYS = Y_DEVICES * ROWS
PAIRS = HEADS // 2
OUTER = 8

NT = (((1,), (1,)), ((), ()))
TN = (((0,), (0,)), ((), ()))
NN = (((1,), (0,)), ((), ()))


def dot(a, b, dims):
    return lax.dot_general(a, b, dims, preferred_element_type=jnp.float32)


def kernel(
    order_ref, q_ref, k_ref, v_ref, o_ref, g_ref, lse_ref,
    dq_ref, dk_ref, dv_ref,
    kv, qs, gs, attn, lse, stat, kpos, weights, own_scores, next_scores, acc, dq_next,
    sx, rx, sy, ry, sq, rq,
    local_sem, z_send, z_recv, ag_send_y, ag_send_own, ag_send_x, ag_recv,
    rs_send_x, rs_recv_x, rs_send_y, rs_recv_y, dq_send, dq_recv,
):
    inner = lax.axis_index("inner")
    outer = lax.axis_index("outer")
    head = lax.axis_index("head")
    x = inner // Y_DEVICES
    y = lax.rem(inner, Y_DEVICES)
    inv_root = 1.0 / math.sqrt(DIM)

    def at_x(distance):
        return (lax.rem(x + distance, X_DEVICES) * Y_DEVICES + y, outer, head)

    def at_y(distance):
        return (x * Y_DEVICES + lax.rem(y + distance, Y_DEVICES), outer, head)

    def at_z(distance):
        return (inner, outer + distance, head)

    def rows_of(xi):
        return pl.ds(pl.multiple_of(xi * ROWS, ROWS), ROWS)

    def block(xi, yi, i):
        return kv.at[yi, i, rows_of(xi), :]

    barrier = pltpu.get_barrier_semaphore()
    for distance in (1, 2, 3):
        pl.semaphore_signal(barrier, inc=1, device_id=at_x(distance), device_id_type=MESH)
        pl.semaphore_signal(barrier, inc=1, device_id=at_y(distance), device_id_type=MESH)

    @pl.when(outer > 0)
    def _():
        pl.semaphore_signal(barrier, inc=1, device_id=at_z(-1), device_id_type=MESH)

    @pl.when(outer < OUTER - 1)
    def _():
        pl.semaphore_signal(barrier, inc=1, device_id=at_z(1), device_id_type=MESH)

    loads = [
        pltpu.make_async_copy(k_ref, kv.at[y, 0, rows_of(x), :], local_sem.at[0]),
        pltpu.make_async_copy(v_ref, kv.at[y, 1, rows_of(x), :], local_sem.at[1]),
        pltpu.make_async_copy(g_ref, gs.at[0], local_sem.at[2]),
        pltpu.make_async_copy(o_ref, attn, local_sem.at[3]),
        pltpu.make_async_copy(lse_ref, lse, local_sem.at[4]),
        pltpu.make_async_copy(q_ref, qs.at[0], local_sem.at[5]),
    ]
    for load in loads:
        load.start()

    peers = 6 + jnp.minimum(outer, 1) + jnp.minimum(OUTER - 1 - outer, 1)
    pl.semaphore_wait(barrier, peers)

    def send_own(i, target, sems, slot):
        return pltpu.make_async_remote_copy(
            (k_ref, v_ref)[i], block(x, y, i), sems.at[slot, i],
            ag_recv.at[x * Y_DEVICES + y, i], device_id=target, device_id_type=MESH,
        )

    def send_y(distance, i):
        return send_own(i, at_y(distance), ag_send_y, distance - 1)

    def send_x(step, distance, i):
        if step == 0:
            return send_own(i, at_x(distance), ag_send_own, distance - 1)
        yi = lax.rem(y + step, Y_DEVICES)
        return pltpu.make_async_remote_copy(
            block(x, yi, i), block(x, yi, i), ag_send_x.at[step - 1, distance - 1, i],
            ag_recv.at[x * Y_DEVICES + yi, i], device_id=at_x(distance), device_id_type=MESH,
        )

    def wait_block(xi, yi, i):
        pltpu.make_async_remote_copy(
            block(xi, yi, i), block(xi, yi, i), ag_send_y.at[0, 0],
            ag_recv.at[xi * Y_DEVICES + yi, i], device_id=at_y(1), device_id_type=MESH,
        ).wait_recv()

    def z_copies():
        return [
            pltpu.make_async_remote_copy(
                source, landing.at[1], z_send.at[i], z_recv.at[i],
                device_id=at_z(-1), device_id_type=MESH,
            )
            for i, (source, landing) in enumerate(((q_ref, qs), (g_ref, gs), (stat.at[0], stat)))
        ]

    @pl.when(outer > 0)
    def _():
        for copy in z_copies()[:2]:
            copy.start()

    for distance in (1, 3, 2):
        for i in (0, 1):
            send_y(distance, i).start()

    for i in (0, 1):
        for distance in (1, 3, 2):
            send_x(0, distance, i).start()

    for load in loads:
        load.wait()

    stat[0, 0, 0:HEADS, :] = lse[...] * LOG2E
    ones = jnp.ones((8, DIM), jnp.bfloat16)
    for h in range(HEADS):
        product = gs[0, h].astype(jnp.float32) * attn[h].astype(jnp.float32)
        high = product.astype(jnp.bfloat16)
        low = (product - high.astype(jnp.float32)).astype(jnp.bfloat16)
        sums = dot(ones, high, NT) + dot(ones, low, NT)
        stat[0, 1, h : h + 1, :] = sums[0:1, :]

    row = lax.broadcasted_iota(jnp.int32, (SPAN, DIM), 0)
    for device in range(X_DEVICES * Y_DEVICES):
        rank = order_ref[device]
        xi, yi = divmod(device, Y_DEVICES)
        kpos[yi, xi * ROWS : xi * ROWS + SPAN, :] = row + rank * SPAN
        kpos[yi, xi * ROWS + SPAN : (xi + 1) * ROWS, :] = (
            row + (2 * X_DEVICES * Y_DEVICES - 1 - rank) * SPAN
        )
    lane = lax.broadcasted_iota(jnp.int32, (1, ROWS), 1)
    rank = order_ref[inner]
    qpos = jnp.where(
        lane < SPAN,
        rank * SPAN + lane,
        (2 * X_DEVICES * Y_DEVICES - 1 - rank) * SPAN + lane - SPAN,
    )
    qpos = jnp.concatenate([qpos, qpos], axis=1)

    @pl.when(outer > 0)
    def _():
        z_copies()[2].start()

    def tile(step, half, scores):
        yi = lax.rem(y + step, Y_DEVICES)
        keys = kv[yi, 0]
        values = kv[yi, 1]
        if half == 0:
            column = kpos[yi]
            column = jnp.concatenate([column, column], axis=1)
        for pair in range(PAIRS):
            two = slice(2 * pair, 2 * pair + 2)
            q_two = qs[half, two].reshape(2 * ROWS, DIM)
            g_two = gs[half, two].reshape(2 * ROWS, DIM)
            norms = jnp.concatenate(
                [stat[half, 0, 2 * pair + i : 2 * pair + i + 1, :] for i in (0, 1)], axis=1
            )
            dots = jnp.concatenate(
                [stat[half, 1, 2 * pair + i : 2 * pair + i + 1, :] for i in (0, 1)], axis=1
            )
            p = jnp.exp2(dot(keys, q_two, NT) * (inv_root * LOG2E) - norms)
            if half == 0:
                p = jnp.where(column <= qpos, p, 0.0)
            lanes = slice(2 * pair * ROWS, 2 * (pair + 1) * ROWS)
            weights[:, lanes] = p.astype(jnp.bfloat16)
            ds = (p * (dot(values, g_two, NT) - dots)).astype(jnp.bfloat16)
            scores[step, :, lanes] = ds

    def key_grad(step, half, i):
        if i == 0:
            scores = (own_scores, next_scores)[half]
            return dot(scores[step], qs[half].reshape(HEADS * ROWS, DIM), NN)
        return dot(weights[...], gs[half].reshape(HEADS * ROWS, DIM), NN)

    def own_tile(step):
        tile(step, 0, own_scores)
        for i in (0, 1):
            acc[step, i] = key_grad(step, 0, i)

    def query_grads(scores, steps):
        total = None
        for step in steps:
            part = dot(scores[step], kv[lax.rem(y + step, Y_DEVICES), 0], TN)
            total = part if total is None else total + part
        return total

    def pass_on(step):
        for i in (0, 1):
            wait_block(x, lax.rem(y + step, Y_DEVICES), i)
            for distance in (1, 3, 2):
                send_x(step, distance, i).start()

    def wait_others(step):
        for i in (0, 1):
            for distance in (1, 3, 2):
                wait_block(lax.rem(x + distance, X_DEVICES), lax.rem(y + step, Y_DEVICES), i)

    def rs_x(step, distance, i):
        xi = lax.rem(x + distance, X_DEVICES)
        return pltpu.make_async_remote_copy(
            sx.at[step, i, rows_of(xi), :], rx.at[step, distance - 1, i],
            rs_send_x.at[step, distance - 1, i], rs_recv_x.at[step, distance - 1, i],
            device_id=at_x(distance), device_id_type=MESH,
        )

    def rs_y(step, i):
        return pltpu.make_async_remote_copy(
            sy.at[step - 1, i], ry.at[step - 1, i], rs_send_y.at[step - 1, i],
            rs_recv_y.at[step - 1, i], device_id=at_y(step), device_id_type=MESH,
        )

    def send_tile(step):
        for i in (0, 1):
            for distance in (2, 1, 3):
                rs_x(step, distance, i).start()

    def next_tile(step, send=True):
        tile(step, 1, next_scores)
        for i in (0, 1):
            grad = acc[step, i] + key_grad(step, 1, i)
            if i == 0:
                grad = grad * inv_root
            acc[step, i] = grad
            sx[step, i] = grad.astype(jnp.bfloat16)
            if send:
                for distance in (2, 1, 3):
                    rs_x(step, distance, i).start()

    def over_x(step, i):
        total = acc[step, i, rows_of(x), :]
        for distance in (1, 2, 3):
            rs_x(step, distance, i).wait_recv()
            total = total + rx[step, distance - 1, i].astype(jnp.float32)
        return total

    def to_y(step):
        for i in (0, 1):
            sy[step - 1, i] = over_x(step, i).astype(jnp.bfloat16)
            rs_y(step, i).start()

    def dq_copy(distance):
        return pltpu.make_async_remote_copy(
            sq, rq, dq_send, dq_recv, device_id=at_z(distance), device_id_type=MESH
        )

    pass_on(1)
    pass_on(3)
    wait_others(0)
    own_tile(0)
    pass_on(2)
    wait_others(1)
    own_tile(1)

    @pl.when(outer < OUTER - 1)
    def _():
        for copy in z_copies():
            copy.wait_recv()

    @pl.when(outer == OUTER - 1)
    def _():
        stat[1] = jnp.zeros_like(stat[1])
        qs[1] = jnp.zeros_like(qs[1])
        gs[1] = jnp.zeros_like(gs[1])

    next_tile(1)
    wait_others(3)
    own_tile(3)
    next_tile(3, False)
    dq_next[...] = query_grads(next_scores, (1, 3))
    wait_others(2)
    own_tile(2)
    next_tile(2)
    send_tile(3)
    to_y(1)
    next_tile(0)
    sq[...] = (
        (dq_next[...] + query_grads(next_scores, (2, 0,))) * inv_root
    ).astype(jnp.bfloat16)

    @pl.when(outer < OUTER - 1)
    def _():
        dq_copy(1).start()

    to_y(2)
    to_y(3)
    totals = [over_x(0, 0), over_x(0, 1)]
    own = query_grads(own_scores, range(Y_DEVICES)) * inv_root

    @pl.when(outer > 0)
    def _():
        dq_copy(-1).wait_recv()

    @pl.when(outer == 0)
    def _():
        rq[...] = jnp.zeros_like(rq)

    dq_ref[...] = (
        (own + rq[...].astype(jnp.float32)).astype(jnp.bfloat16).reshape(HEADS, ROWS, DIM)
    )

    for i in (0, 1):
        total = totals[i]
        for step in (1, 3, 2):
            rs_y(step, i).wait_recv()
            total = total + ry[step - 1, i].astype(jnp.float32)
        (dk_ref, dv_ref)[i][...] = total.astype(jnp.bfloat16)

    for i in (0, 1):
        for distance in (1, 2, 3):
            send_y(distance, i).wait_send()
            rs_y(distance, i).wait_send()
            for step in range(Y_DEVICES):
                send_x(step, distance, i).wait_send()
                rs_x(step, distance, i).wait_send()

    @pl.when(outer > 0)
    def _():
        for copy in z_copies():
            copy.wait_send()

    @pl.when(outer < OUTER - 1)
    def _():
        dq_copy(1).wait_send()


def store_kernel(dq_in, dk_in, dv_in, dq_ref, dk_ref, dv_ref, sems):
    copies = [
        pltpu.make_async_copy(dq_in, dq_ref, sems.at[0]),
        pltpu.make_async_copy(dk_in, dk_ref, sems.at[1]),
        pltpu.make_async_copy(dv_in, dv_ref, sems.at[2]),
    ]
    for copy in copies:
        copy.start()
    for copy in copies:
        copy.wait()


def on_device(queries, key_rows, value_rows, attn_out, grad_out, log_norms, pair_order):
    def heads_first(rows):
        return jnp.transpose(rows, (1, 0, 2))

    half = jnp.bfloat16
    full = jnp.float32
    dma = pltpu.SemaphoreType.DMA
    vmem = pl.BlockSpec(memory_space=pltpu.VMEM)
    hbm = pl.BlockSpec(memory_space=pltpu.HBM)
    grads = (
        jax.ShapeDtypeStruct((HEADS, ROWS, DIM), half),
        jax.ShapeDtypeStruct((ROWS, DIM), half),
        jax.ShapeDtypeStruct((ROWS, DIM), half),
    )
    parts = pl.pallas_call(
        kernel,
        out_shape=tuple(pltpu.VMEM(grad.shape, grad.dtype) for grad in grads),
        in_specs=[pl.BlockSpec(memory_space=pltpu.SMEM), hbm, hbm, hbm, hbm, hbm, hbm],
        out_specs=(vmem, vmem, vmem),
        scratch_shapes=[
            pltpu.VMEM((Y_DEVICES, 2, GROUP_KEYS, DIM), half),
            pltpu.VMEM((2, HEADS, ROWS, DIM), half),
            pltpu.VMEM((2, HEADS, ROWS, DIM), half),
            pltpu.VMEM((HEADS, ROWS, DIM), half),
            pltpu.VMEM((HEADS, ROWS), full),
            pltpu.VMEM((2, 2, 8, ROWS), full),
            pltpu.VMEM((Y_DEVICES, GROUP_KEYS, DIM), jnp.int32),
            pltpu.VMEM((GROUP_KEYS, HEADS * ROWS), half),
            pltpu.VMEM((Y_DEVICES, GROUP_KEYS, HEADS * ROWS), half),
            pltpu.VMEM((Y_DEVICES, GROUP_KEYS, HEADS * ROWS), half),
            pltpu.VMEM((Y_DEVICES, 2, GROUP_KEYS, DIM), full),
            pltpu.VMEM((HEADS * ROWS, DIM), full),
            pltpu.VMEM((Y_DEVICES, 2, GROUP_KEYS, DIM), half),
            pltpu.VMEM((Y_DEVICES, 3, 2, ROWS, DIM), half),
            pltpu.VMEM((3, 2, ROWS, DIM), half),
            pltpu.VMEM((3, 2, ROWS, DIM), half),
            pltpu.VMEM((HEADS * ROWS, DIM), half),
            pltpu.VMEM((HEADS * ROWS, DIM), half),
            dma((6,)), dma((3,)), dma((3,)), dma((3, 2)), dma((3, 2)), dma((3, 3, 2)),
            dma((16, 2)), dma((4, 3, 2)), dma((4, 3, 2)), dma((3, 2)), dma((3, 2)), dma, dma,
        ],
        compiler_params=pltpu.CompilerParams(
            collective_id=0, has_side_effects=True, vmem_limit_bytes=60 * 2**20
        ),
        cost_estimate=pl.CostEstimate(
            flops=4 * 10**9, bytes_accessed=10**6, transcendentals=3 * 10**6
        ),
    )(
        pair_order,
        heads_first(queries),
        key_rows.reshape(ROWS, DIM),
        value_rows.reshape(ROWS, DIM),
        heads_first(attn_out),
        heads_first(grad_out),
        log_norms,
    )
    grad_queries, grad_keys, grad_values = pl.pallas_call(
        store_kernel,
        out_shape=grads,
        in_specs=[vmem, vmem, vmem],
        out_specs=(hbm, hbm, hbm),
        scratch_shapes=[dma((3,))],
        compiler_params=pltpu.CompilerParams(vmem_limit_bytes=2**20),
    )(*parts)
    return (
        jnp.transpose(grad_queries, (1, 0, 2)),
        grad_keys.reshape(ROWS, 1, DIM),
        grad_values.reshape(ROWS, 1, DIM),
    )


def solution(mesh):
    rows = P(("outer", "inner"), "head", None)
    return jax.shard_map(
        on_device,
        mesh=mesh,
        in_specs=(rows, rows, rows, rows, rows, P("head", ("outer", "inner")), P()),
        out_specs=(rows, rows, rows),
        check_vma=False,
    )
```
